256 devices in a mesh: attn: 16 (over y_lo, x, core), ffn: 8 (over z), grp: 2 (over y_hi).
Axes of the slice: x: 4, y: 4 (y_hi: 2, y_lo: 2; y = y_hi * 2 + y_lo), z: 8, core: 2. Of those that a mesh axis runs over, the one named last changes fastest.
Arguments:
- query: bfloat16 [2048, 8192], P(('grp', 'attn'), 'ffn'), parts along dimension 0, may hold values from -5 to 5
- key_store_cache: bfloat16 [2048, 192, 1024], P(('grp', 'attn'), None, 'ffn'), parts along dimension 0, may hold values from -5 to 5
- value_store_cache: bfloat16 [2048, 192, 1024], P(('grp', 'attn'), None, 'ffn'), parts along dimension 0, may hold values from -5 to 5
- token_keys: bfloat16 [2048, 1024], P(('grp', 'attn'), 'ffn'), parts along dimension 0, may hold values from -5 to 5
- token_values: bfloat16 [2048, 1024], P(('grp', 'attn'), 'ffn'), parts along dimension 0, may hold values from -5 to 5
- pooled_block_keys: bfloat16 [512, 16, 1024], P(('grp', 'attn'), None, 'ffn'), parts along dimension 0, may hold values from -5 to 5
- pooled_block_values: bfloat16 [512, 16, 1024], P(('grp', 'attn'), None, 'ffn'), parts along dimension 0, may hold values from -6 to 6
- block_dst: int32 [512, 1], P('grp'), parts along dimension 0, may hold values from 0 to 15; in each aligned block of 16 rows (0 to 15, 16 to 31, ...) at most 2 rows name the same one
- block_row: int32 [512], P('grp'), parts along dimension 0, may hold values from 0 to 63
- ctx_len: int32 [2048], P(('grp', 'attn')), parts along dimension 0, may hold values from 1 to 192, as said below
- residual: bfloat16 [2048, 8192], P('grp', 'attn'), parts along dimension 0, may hold values from -15 to 15
- norm_gain: float32 [8192], P('attn'), may hold values from 0.1 to 1.9
- output_weight: bfloat16 [8192, 8192], P('ffn', 'attn'), may hold values from -0.1875 to 0.1875
- w_gate: bfloat16 [8192, 14336], P('attn', 'ffn'), may hold values from -0.0625 to 0.0625
- w_up: bfloat16 [8192, 14336], P('attn', 'ffn'), may hold values from -0.0625 to 0.0625
- w_down: bfloat16 [14336, 8192], P('ffn', 'attn'), may hold values from -0.046875 to 0.046875
Outputs:
- layer_out: bfloat16 [2048, 8192], P(('grp', 'ffn'), 'attn'), parts along dimension 0
The draws below stay inside these ranges and needn't reach their ends.
There are 2 independent parts, one for each index of `grp`. The reference program is written for one: setup_inputs(seed, part) draws one part's arguments, and reference() takes and returns one part's arrays. A program takes and returns all parts, laid end to end along the dimension named above; an argument that names none is the same for every part. Nothing has to cross between parts.
Inputs may be any that keep to these rules, and one draw needn't show every extreme that they name: `block_dst`: of the 16 blocks held by one pool index (aligned blocks of rows), at most 2 name the same attention index. `ctx_len`: every attention index holds a request that uses all 192 cached positions.
All inputs are finite; a program needn't handle non-finite values.
Results may differ from the reference program's by a relative error of at most 0.024.
Values may be sent and summed in bfloat16 or wider, within the bound.
No kernel may reach another device: no remote copies, remote signals or barrier semaphores. Data moves between devices by JAX's collectives and lax.ppermute only.
A program may use at most 128 MiB of HBM per device.

```python
import math
import jax
import jax.numpy as jnp
import numpy as np
from jax import lax

MODEL_WIDTH = 8192
QUERY_HEADS = 64
KEY_VALUE_HEADS = 8
HEAD_SIZE = 128
FF = 14336
QUERIES_PER_KEY = 8
REQUESTS_PER_IDX = 64
CONTEXT_SLOTS = 192
RESUMED_TOKENS = 16
CAP = 2
RES_DEV = 16
REQUEST_COUNT = 1024
POOL_BLOCKS = 256
N_ATTN = 16
N_FFN = 8


def chosen_rows(key):
    return jax.random.randint(jax.random.fold_in(key, 101), (N_ATTN,), 0, REQUESTS_PER_IDX)


def draw_query(key, part):
    self_key = jax.random.fold_in(key, 5)
    value_rows = jnp.clip(jax.random.normal(self_key, (REQUEST_COUNT, QUERY_HEADS * HEAD_SIZE), jnp.float32), -5.0, 5.0)
    return value_rows.astype(jnp.bfloat16)


def draw_key_store_cache(key, part):
    self_key = jax.random.fold_in(key, 6)
    value_rows = jnp.clip(jax.random.normal(self_key, (REQUEST_COUNT, CONTEXT_SLOTS, KEY_VALUE_HEADS * HEAD_SIZE), jnp.float32), -5.0, 5.0)
    return value_rows.astype(jnp.bfloat16)


def draw_ctx_len(key, part):
    special = chosen_rows(key)
    self_key = jax.random.fold_in(key, 7)
    first_key, second_key = jax.random.split(self_key)
    device_top = jax.random.randint(first_key, (N_ATTN, 1), max(CONTEXT_SLOTS // 4, 1), CONTEXT_SLOTS + 1)
    lengths = jax.random.randint(second_key, (N_ATTN, REQUESTS_PER_IDX), 1, device_top + 1)
    lengths = jnp.where(jnp.arange(REQUESTS_PER_IDX)[None, :] == special[:, None], CONTEXT_SLOTS, lengths)
    return lengths.reshape(REQUEST_COUNT).astype(jnp.int32)


def draw_residual(key, part):
    self_key = jax.random.fold_in(key, 9)
    first_key = jax.random.fold_in(self_key, 0)
    second_key = jax.random.fold_in(self_key, 1)
    fourth_key = jax.random.fold_in(self_key, 3)
    columns = jnp.arange(MODEL_WIDTH, dtype=jnp.float32) / MODEL_WIDTH
    row_scale = jnp.exp(jax.random.uniform(first_key, (REQUEST_COUNT, 1), jnp.float32, math.log(0.2), math.log(2.0)))
    column_scale = 3.0 ** (0.5 * columns) * jnp.exp(jax.random.uniform(second_key, (MODEL_WIDTH,), jnp.float32, -0.5, 0.5))
    base = jnp.clip(jax.random.normal(fourth_key, (REQUEST_COUNT, MODEL_WIDTH), jnp.float32), -2.5, 2.5)
    return (base * row_scale * column_scale[None, :]).astype(jnp.bfloat16)


def with_ends(values, own_key, low, top_value):
    longest = values.shape.index(max(values.shape))
    spots = []
    for shift in (0, 1):
        where = [jax.random.randint(jax.random.fold_in(own_key, axis), (), 0, length) for axis, length in enumerate(values.shape)]
        where[longest] = (where[longest] + shift) % values.shape[longest]
        spots.append(tuple(where))
    return values.at[spots[0]].set(low).at[spots[1]].set(top_value)


def block_scale(own_key, shape, shards, smallest, largest):
    def one(dim, parts):
        steps = jax.random.uniform(jax.random.fold_in(jax.random.fold_in(own_key, 6), dim), (parts,), jnp.float32, smallest / len(shards), largest / len(shards))
        return jnp.repeat(jnp.exp(steps), shape[dim] // parts).reshape((-1,) + (1,) * (len(shape) - dim - 1))

    level = one(*shards[0])
    for cut in shards[1:]:
        level = level * one(*cut)
    return level


def routed_block(stream_key, own, number, rows, number_of, top, bound, skew):
    order = jax.random.permutation(stream_key, number_of)
    packed, usual = load_shares(number_of, rows * top, bound, skew, True), load_shares(number_of, rows * top, bound, skew, False)
    places = jnp.arange(number_of)

    def named(tallies, rotation):
        used = int((tallies > 0).sum())
        fixed = max(1, used // 4)
        moved = fixed + (places - fixed + rotation * (used - fixed)) % max(1, number_of - fixed)
        return jnp.zeros((number_of,), jnp.int32).at[order[jnp.where(places < fixed, places, moved)]].set(jnp.asarray(tallies, jnp.int32))

    tallies = jnp.where(number % 4 == 0, named(packed, number // 4), named(usual, number - number // 4 - 1))
    mixed = jax.random.permutation(jax.random.fold_in(own, 3), number_of)
    giver, sink = mixed[0:number_of // 2 * 2:2], mixed[1:number_of // 2 * 2:2]
    slack = jnp.minimum(tallies[giver] - 1, bound - tallies[sink]) // 2
    slack = jnp.where((giver == order[0]) | (sink == order[0]) | (tallies[sink] == 0), 0, jnp.maximum(slack, 0))
    moved = jax.random.randint(jax.random.fold_in(own, 4), (number_of // 2,), 0, 1 << 20) % (slack + 1)
    tallies = tallies.at[giver].add(-moved).at[sink].add(moved)
    members = jnp.searchsorted(jnp.cumsum(tallies), jnp.arange(rows * top), side="right").astype(jnp.int32)
    table = members.reshape(top, rows).T
    table = table[jax.random.permutation(jax.random.fold_in(own, 1), rows)]
    rotation = jax.random.randint(jax.random.fold_in(own, 2), (rows, 1), 0, top)
    return jnp.take_along_axis(table, (jnp.arange(top)[None, :] + rotation) % top, axis=1)


def load_shares(amount, total, limit, skew, full):
    portions = [(1 << 20) // math.isqrt(standing ** skew) + 1 for standing in range(1, amount + 1)]
    largest = limit if full else min(limit, max(-(-total // amount), total * portions[0] // sum(portions)))
    least = 1 if total - largest >= amount - 1 else 0
    given, rest = [largest] + [least] * (amount - 1), total - largest - least * (amount - 1)
    while rest > 0:
        free = [i for i in range(1, amount) if given[i] < largest] or [i for i in range(1, amount) if given[i] < limit]
        mass, budget = sum([portions[i] for i in free]), rest
        for i in free:
            more = min(limit - given[i], max(1, budget * portions[i] // mass), rest)
            given[i] = given[i] + more
            rest = rest - more
    return np.array(given)


def scatter_about(key, extent, width, most, pieces=(), kind=jnp.bfloat16):
    entries = width * jax.random.normal(key, extent, jnp.float32)
    if pieces:
        entries = entries * block_scale(key, extent, pieces, -0.22, 0.18)
    return jnp.clip(entries, -most, most).astype(kind)


def setup_inputs(seed: int = 0, part: int = 0) -> dict:
    streams_of = jax.random.split(jax.random.key(seed), 17)
    part_splits = jax.random.split(jax.random.fold_in(streams_of[16], part), 17)
    query = draw_query(jax.random.fold_in(jax.random.fold_in(streams_of[16], part), 71), part)
    key_store_cache = draw_key_store_cache(jax.random.fold_in(jax.random.fold_in(streams_of[16], part), 71), part)
    value_store_cache = scatter_about(part_splits[2], (REQUEST_COUNT, CONTEXT_SLOTS, KEY_VALUE_HEADS * HEAD_SIZE), 1.0, 5.0, ((0, 16), (2, 8)))
    token_keys = scatter_about(part_splits[3], (REQUEST_COUNT, KEY_VALUE_HEADS * HEAD_SIZE), 1.0, 5.0, ((0, 16), (1, 8)))
    token_values = scatter_about(part_splits[4], (REQUEST_COUNT, KEY_VALUE_HEADS * HEAD_SIZE), 1.0, 5.0, ((0, 16), (1, 8)))
    pooled_block_keys = scatter_about(part_splits[5], (POOL_BLOCKS, RESUMED_TOKENS, KEY_VALUE_HEADS * HEAD_SIZE), 1.0, 5.0, ((0, 16), (2, 8)))
    pooled_block_values = scatter_about(part_splits[6], (POOL_BLOCKS, RESUMED_TOKENS, KEY_VALUE_HEADS * HEAD_SIZE), 1.5, 6.0, ((0, 16), (2, 8)))
    block_dst_keys = jax.random.split(jax.random.fold_in(part_splits[7], 1), POOL_BLOCKS // RES_DEV)
    block_dst_turns = jax.random.permutation(jax.random.fold_in(part_splits[7], 3), POOL_BLOCKS // RES_DEV)
    block_dst = jax.vmap(lambda own, number: routed_block(jax.random.fold_in(part_splits[7], 2), own, number, RES_DEV, N_ATTN, 1, CAP, 2))(block_dst_keys, block_dst_turns).reshape((POOL_BLOCKS, 1))
    block_row = with_ends(jax.random.randint(part_splits[8], (POOL_BLOCKS,), 0, REQUESTS_PER_IDX), jax.random.fold_in(part_splits[8], 1), 0, REQUESTS_PER_IDX - 1).astype(jnp.int32)
    ctx_len = draw_ctx_len(jax.random.fold_in(jax.random.fold_in(streams_of[16], part), 71), part)
    residual = draw_residual(jax.random.fold_in(jax.random.fold_in(streams_of[16], part), 71), part)
    norm_gain = jnp.clip(1.0 + 0.18 * jax.random.normal(streams_of[11], (MODEL_WIDTH,), jnp.float32), 0.1, 1.9)
    output_weight = scatter_about(streams_of[12], (QUERY_HEADS * HEAD_SIZE, MODEL_WIDTH), (KEY_VALUE_HEADS * HEAD_SIZE) ** -0.5, 0.1875, ((0, 8), (1, 16)))
    w_gate = scatter_about(streams_of[13], (MODEL_WIDTH, FF), MODEL_WIDTH ** -0.5, 0.0625, ((0, 16), (1, 8)))
    w_up = scatter_about(streams_of[14], (MODEL_WIDTH, FF), MODEL_WIDTH ** -0.5, 0.0625, ((0, 16), (1, 8)))
    w_down = scatter_about(streams_of[15], (FF, MODEL_WIDTH), FF ** -0.5, 0.046875, ((0, 8), (1, 16)))
    return {"query": query, "key_store_cache": key_store_cache, "value_store_cache": value_store_cache, "token_keys": token_keys, "token_values": token_values, "pooled_block_keys": pooled_block_keys, "pooled_block_values": pooled_block_values, "block_dst": block_dst, "block_row": block_row, "ctx_len": ctx_len, "residual": residual, "norm_gain": norm_gain, "output_weight": output_weight, "w_gate": w_gate, "w_up": w_up, "w_down": w_down}


epsilon = 1e-05

def rounded(value):
    return lax.optimization_barrier(value.astype(jnp.bfloat16)).astype(jnp.float32)

def reference(query, key_store_cache, value_store_cache, token_keys, token_values, pooled_block_keys, pooled_block_values, block_dst, block_row, ctx_len, residual, norm_gain, output_weight, w_gate, w_up, w_down):
    score_scale = HEAD_SIZE ** (-0.5)
    gathered_keys = pooled_block_keys.astype(jnp.float32).reshape(POOL_BLOCKS * RESUMED_TOKENS, KEY_VALUE_HEADS, HEAD_SIZE)
    gathered_values = pooled_block_values.astype(jnp.float32).reshape(POOL_BLOCKS * RESUMED_TOKENS, KEY_VALUE_HEADS, HEAD_SIZE)
    local_rows = jnp.arange(REQUESTS_PER_IDX, dtype=jnp.int32)

    def attend(index):
        leading_entry = index * REQUESTS_PER_IDX
        query_rows = lax.dynamic_slice_in_dim(query, leading_entry, REQUESTS_PER_IDX, 0).astype(jnp.float32).reshape(REQUESTS_PER_IDX, KEY_VALUE_HEADS, QUERIES_PER_KEY, HEAD_SIZE)
        stored_keys = lax.dynamic_slice_in_dim(key_store_cache, leading_entry, REQUESTS_PER_IDX, 0).astype(jnp.float32).reshape(REQUESTS_PER_IDX, CONTEXT_SLOTS, KEY_VALUE_HEADS, HEAD_SIZE)
        stored_values = lax.dynamic_slice_in_dim(value_store_cache, leading_entry, REQUESTS_PER_IDX, 0).astype(jnp.float32).reshape(REQUESTS_PER_IDX, CONTEXT_SLOTS, KEY_VALUE_HEADS, HEAD_SIZE)
        current_keys = lax.dynamic_slice_in_dim(token_keys, leading_entry, REQUESTS_PER_IDX, 0).astype(jnp.float32).reshape(REQUESTS_PER_IDX, KEY_VALUE_HEADS, HEAD_SIZE)
        current_values = lax.dynamic_slice_in_dim(token_values, leading_entry, REQUESTS_PER_IDX, 0).astype(jnp.float32).reshape(REQUESTS_PER_IDX, KEY_VALUE_HEADS, HEAD_SIZE)
        lengths = lax.dynamic_slice_in_dim(ctx_len, leading_entry, REQUESTS_PER_IDX, 0)
        score_cache = jnp.einsum('bghd,btgd->bght', query_rows, stored_keys) * score_scale
        valid_mask = jnp.arange(CONTEXT_SLOTS, dtype=jnp.int32)[None, :] < lengths[:, None]
        score_cache = jnp.where(valid_mask[:, None, None, :], score_cache, -jnp.inf)
        score_pool = jnp.einsum('bghd,tgd->bght', query_rows, gathered_keys) * score_scale
        owner_mask = (block_dst[:, 0] == index)[None, :] & (block_row[None, :] == local_rows[:, None])
        owner_mask = jnp.repeat(owner_mask, RESUMED_TOKENS, axis=1)
        score_pool = jnp.where(owner_mask[:, None, None, :], score_pool, -jnp.inf)
        score_new = jnp.einsum('bghd,bgd->bgh', query_rows, current_keys) * score_scale
        row_max = jnp.maximum(jnp.maximum(lax.optimization_barrier(jnp.max(score_cache, axis=-1)), lax.optimization_barrier(jnp.max(score_pool, axis=-1))), score_new)
        exp_cache = jnp.exp(score_cache - row_max[..., None])
        exp_pool = jnp.exp(score_pool - row_max[..., None])
        exp_new = jnp.exp(score_new - row_max)
        denominator = lax.optimization_barrier(jnp.sum(exp_cache, axis=-1)) + lax.optimization_barrier(jnp.sum(exp_pool, axis=-1)) + exp_new
        prob_cache = (exp_cache / denominator[..., None]).astype(jnp.bfloat16).astype(jnp.float32)
        prob_pool = (exp_pool / denominator[..., None]).astype(jnp.bfloat16).astype(jnp.float32)
        prob_new = (exp_new / denominator).astype(jnp.bfloat16).astype(jnp.float32)
        weighted = jnp.einsum('bght,btgd->bghd', prob_cache, stored_values)
        weighted = weighted + jnp.einsum('bght,tgd->bghd', prob_pool, gathered_values)
        weighted = weighted + prob_new[..., None] * current_values[:, :, None, :]
        return weighted.reshape(REQUESTS_PER_IDX, QUERY_HEADS * HEAD_SIZE).astype(jnp.bfloat16)
    attended = lax.map(attend, jnp.arange(N_ATTN, dtype=jnp.int32)).reshape(REQUEST_COUNT, QUERY_HEADS * HEAD_SIZE)
    head_cols = QUERY_HEADS * HEAD_SIZE // N_FFN
    attn_out = jnp.zeros((REQUEST_COUNT, MODEL_WIDTH), jnp.float32)
    for index in range(N_FFN):
        part_sum = jnp.dot(attended[:, index * head_cols:(index + 1) * head_cols], output_weight[index * head_cols:(index + 1) * head_cols], preferred_element_type=jnp.float32)
        attn_out = attn_out + rounded(part_sum)
    mixed = residual.astype(jnp.float32) + attn_out
    inverse = lax.rsqrt(lax.optimization_barrier(jnp.mean(mixed * mixed, axis=1)) + epsilon)
    normed = (mixed * inverse[:, None] * norm_gain).astype(jnp.bfloat16)
    width_cols = MODEL_WIDTH // N_ATTN
    gate = jnp.zeros((REQUEST_COUNT, FF), jnp.float32)
    up_sum = jnp.zeros((REQUEST_COUNT, FF), jnp.float32)
    for index in range(N_ATTN):
        segment = normed[:, index * width_cols:(index + 1) * width_cols]
        gate = gate + rounded(jnp.dot(segment, w_gate[index * width_cols:(index + 1) * width_cols], preferred_element_type=jnp.float32))
        up_sum = up_sum + rounded(jnp.dot(segment, w_up[index * width_cols:(index + 1) * width_cols], preferred_element_type=jnp.float32))
    activated = (jax.nn.silu(gate) * up_sum).astype(jnp.bfloat16)
    hidden_cols = FF // N_FFN
    ffn_out = jnp.zeros((REQUEST_COUNT, MODEL_WIDTH), jnp.float32)
    for index in range(N_FFN):
        part_sum = jnp.dot(activated[:, index * hidden_cols:(index + 1) * hidden_cols], w_down[index * hidden_cols:(index + 1) * hidden_cols], preferred_element_type=jnp.float32)
        ffn_out = ffn_out + rounded(part_sum)
    return (mixed + ffn_out).astype(jnp.bfloat16)
```

```python
import jax
import jax.numpy as jnp
from jax import lax
from jax.experimental import pallas as pl
from jax.experimental.pallas import tpu as pltpu
from jax.sharding import PartitionSpec as P

MODEL_WIDTH = 8192
HEAD_SIZE = 128
HEADS = 8
CAP = 2
CHIPS = 8
epsilon = 1e-05
BF = jnp.bfloat16
F32 = jnp.float32
VMEM_BYTES = 40 * 1024 * 1024
NT = (((1,), (1,)), ((), ()))


def params():
    return pltpu.CompilerParams(vmem_limit_bytes=VMEM_BYTES)


def whole(shape):
    return pl.BlockSpec(shape, lambda *_: (0,) * len(shape))


def cost(flops, size):
    return pl.CostEstimate(flops=flops, bytes_accessed=size, transcendentals=0)


def swap_core(value):
    return lax.ppermute(value, "attn", [(a, a ^ 1) for a in range(16)])


def exchange_chips(value):
    groups = [[2 * k + c for k in range(CHIPS)] for c in range(2)]
    return lax.all_to_all(
        value, "attn", split_axis=0, concat_axis=0, axis_index_groups=groups, tiled=True
    )


def z_shift(value, step):
    return lax.ppermute(value, "ffn", [(f, (f + step) % 8) for f in range(8)])


def z_scatter_sum(take):
    right, left = take(4), take(-3)
    for step in range(1, 5):
        right = z_shift(right, 1)
        if step < 4:
            right = (right.astype(F32) + take(4 - step).astype(F32)).astype(BF)
            left = z_shift(left, -1)
            if step < 3:
                left = (left.astype(F32) + take(step - 3).astype(F32)).astype(BF)
    return right.astype(F32) + left.astype(F32) + take(0).astype(F32)


def z_gather(value):
    right = left = value
    blocks = [None] * 8
    blocks[0] = value
    for step in range(1, 5):
        right = z_shift(right, 1)
        blocks[8 - step] = right
        if step < 4:
            left = z_shift(left, -1)
            blocks[step] = left
    return blocks


def place_blocks(block_dst, pooled_keys, pooled_values):
    held, block_len, width = pooled_keys.shape
    slots = 16 * CAP

    def kernel(dst_ref, k_ref, v_ref, out_ref):
        first = lax.axis_index("attn") * held
        out_ref[...] = jnp.zeros_like(out_ref)
        dst = [dst_ref[first + j] for j in range(held)]
        for j in range(held):
            rank = jnp.int32(0)
            for i in range(j):
                rank = rank + jnp.where(dst[i] == dst[j], 1, 0)
            slot = dst[j] * CAP + jnp.minimum(rank, CAP - 1)
            out_ref[slot, :, :width] = k_ref[j]
            out_ref[slot, :, width:] = v_ref[j]

    return pl.pallas_call(
        kernel,
        out_shape=jax.ShapeDtypeStruct((slots, block_len, 2 * width), BF),
        in_specs=[
            pl.BlockSpec(memory_space=pltpu.SMEM),
            pl.BlockSpec(memory_space=pltpu.VMEM),
            pl.BlockSpec(memory_space=pltpu.VMEM),
        ],
        out_specs=pl.BlockSpec(memory_space=pltpu.VMEM),
        compiler_params=params(),
    )(block_dst, pooled_keys, pooled_values)


def attention(ctx_len, query, keys, values, token_keys, token_values, received, dst, rows):
    requests, ctx_size, width = keys.shape
    step_rows = 16
    slots = 16 * CAP
    block_len = received.shape[0] // slots
    recv_size = received.shape[0]
    scale = HEAD_SIZE**-0.5
    hrows = step_rows * HEADS

    def kernel(
        ctx_ref, q_ref, k_ref, v_ref, tk_ref, tv_ref, r_ref, dst_ref, row_ref,
        out_ref, owner_ref, q_buf, tk_buf, tv_buf, o_buf,
    ):
        step = pl.program_id(0)

        @pl.when(step == 0)
        def _():
            me = lax.axis_index("attn")
            hit = dst_ref[...] == me
            hit_f = hit.astype(F32)
            count = hit.shape[1]
            before = lax.broadcasted_iota(jnp.int32, (count, count), 0) < lax.broadcasted_iota(
                jnp.int32, (count, count), 1
            )
            rank = jnp.dot(hit_f, before.astype(F32), preferred_element_type=F32)
            marked = row_ref[...].astype(F32) + 1.0
            first = jnp.sum(jnp.where(hit & (rank < 0.5), marked, 0.0), axis=1, keepdims=True)
            second = jnp.sum(
                jnp.where(hit & (rank > 0.5) & (rank < 1.5), marked, 0.0), axis=1, keepdims=True
            )
            slot = lax.broadcasted_iota(jnp.int32, (16, recv_size), 1) // block_len
            pool = lax.broadcasted_iota(jnp.int32, (16, recv_size), 0)
            found = jnp.where(slot == pool * CAP, first, 0.0) + jnp.where(
                slot == pool * CAP + 1, second, 0.0
            )
            owner_ref[...] = jnp.broadcast_to(
                jnp.sum(found, axis=0, keepdims=True) - 1.0, owner_ref.shape
            )

        for h in range(HEADS):
            q_buf[pl.ds(h, step_rows, stride=HEADS), :] = q_ref[
                :, h * HEAD_SIZE : (h + 1) * HEAD_SIZE
            ].astype(F32)
            tk_buf[pl.ds(h, step_rows, stride=HEADS), :] = tk_ref[...].astype(F32)
            tv_buf[pl.ds(h, step_rows, stride=HEADS), :] = tv_ref[...].astype(F32)
        q_full = q_buf[...]
        q_half = q_full.astype(BF)
        scores = []
        spot = lax.broadcasted_iota(jnp.int32, (HEADS, ctx_size), 1)
        for b in range(step_rows):
            part = lax.dot_general(
                q_half[b * HEADS : (b + 1) * HEADS], k_ref[b], NT, preferred_element_type=F32
            )
            scores.append(
                jnp.where(spot < ctx_ref[step * step_rows + b], part * scale, -jnp.inf)
            )
        score_cache = jnp.concatenate(scores, axis=0)
        score_recv = (
            lax.dot_general(q_half, r_ref[:, :width], NT, preferred_element_type=F32) * scale
        )
        request = (
            lax.broadcasted_iota(jnp.int32, (hrows, recv_size), 0) // HEADS + step * step_rows
        )
        score_recv = jnp.where(request.astype(F32) == owner_ref[0:1, :], score_recv, -jnp.inf)
        score_new = jnp.sum(q_full * tk_buf[...], axis=1, keepdims=True) * scale
        top = jnp.maximum(
            jnp.maximum(
                jnp.max(score_cache, axis=1, keepdims=True),
                jnp.max(score_recv, axis=1, keepdims=True),
            ),
            score_new,
        )
        exp_cache = jnp.exp(score_cache - top)
        exp_recv = jnp.exp(score_recv - top)
        exp_new = jnp.exp(score_new - top)
        total = (
            jnp.sum(exp_cache, axis=1, keepdims=True)
            + jnp.sum(exp_recv, axis=1, keepdims=True)
            + exp_new
        )
        inverse = 1.0 / total
        prob_cache = (exp_cache * inverse).astype(BF)
        prob_recv = (exp_recv * inverse).astype(BF)
        prob_new = (exp_new * inverse).astype(BF).astype(F32)
        attended = [
            jnp.dot(
                prob_cache[b * HEADS : (b + 1) * HEADS], v_ref[b], preferred_element_type=F32
            )
            for b in range(step_rows)
        ]
        o_buf[...] = (
            jnp.concatenate(attended, axis=0)
            + jnp.dot(prob_recv, r_ref[:, width:], preferred_element_type=F32)
            + prob_new * tv_buf[...]
        )
        for h in range(HEADS):
            head = o_buf[pl.ds(h, step_rows, stride=HEADS), :].astype(BF)
            out_ref[:, :, h * HEAD_SIZE : (h + 1) * HEAD_SIZE] = jnp.broadcast_to(
                head[None], (CHIPS, step_rows, HEAD_SIZE)
            )

    return pl.pallas_call(
        kernel,
        grid=(requests // step_rows,),
        out_shape=jax.ShapeDtypeStruct((CHIPS, requests, query.shape[1]), BF),
        in_specs=[
            pl.BlockSpec(memory_space=pltpu.SMEM),
            pl.BlockSpec((step_rows, query.shape[1]), lambda i: (i, 0)),
            pl.BlockSpec((step_rows, ctx_size, width), lambda i: (i, 0, 0)),
            pl.BlockSpec((step_rows, ctx_size, width), lambda i: (i, 0, 0)),
            pl.BlockSpec((step_rows, width), lambda i: (i, 0)),
            pl.BlockSpec((step_rows, width), lambda i: (i, 0)),
            whole(received.shape),
            whole(dst.shape),
            whole(rows.shape),
        ],
        out_specs=pl.BlockSpec((CHIPS, step_rows, query.shape[1]), lambda i: (0, i, 0)),
        scratch_shapes=[
            pltpu.VMEM((8, recv_size), F32),
            pltpu.VMEM((hrows, HEAD_SIZE), F32),
            pltpu.VMEM((hrows, HEAD_SIZE), F32),
            pltpu.VMEM((hrows, HEAD_SIZE), F32),
            pltpu.VMEM((hrows, HEAD_SIZE), F32),
        ],
        compiler_params=params(),
        cost_estimate=cost(10**8, 7 * 10**6),
    )(ctx_len, query, keys, values, token_keys, token_values, received, dst, rows)


def side_by_side(x, near, far, tile=256):
    m, k = x.shape
    n = near.shape[1]
    steps = n // tile

    def kernel(x_ref, near_ref, far_ref, out_ref):
        step = pl.program_id(0)

        @pl.when(step < steps)
        def _():
            out_ref[...] = jnp.dot(x_ref[...], near_ref[...], preferred_element_type=F32).astype(BF)

        @pl.when(step >= steps)
        def _():
            out_ref[...] = jnp.dot(x_ref[...], far_ref[...], preferred_element_type=F32).astype(BF)

    return pl.pallas_call(
        kernel,
        grid=(2 * steps,),
        out_shape=jax.ShapeDtypeStruct((m, 2 * n), BF),
        in_specs=[
            whole(x.shape),
            pl.BlockSpec((k, tile), lambda j: (0, jnp.minimum(j, steps - 1))),
            pl.BlockSpec((k, tile), lambda j: (0, jnp.maximum(j - steps, 0))),
        ],
        out_specs=pl.BlockSpec((m, tile), lambda j: (0, j)),
        compiler_params=params(),
        cost_estimate=cost(4 * m * n * k, 4 * (m * k + k * n)),
    )(x, near, far)


def gate_up(blocks, gains, gates, ups, tile=256):
    count = len(blocks)
    rows, width = blocks[0].shape
    part = width // len(gates)
    hidden = gates[0].shape[1]
    steps = hidden // tile
    full = 2 * hidden + 128

    def kernel(*refs):
        block_refs = refs[:count]
        gain_refs = refs[count : count + 2]
        gate_refs = refs[count + 2 : count + 4]
        up_refs = refs[count + 4 : count + 6]
        out_ref, x_ref = refs[count + 6 :]
        step = pl.program_id(0)

        @pl.when(step == 0)
        def _():
            gain = jnp.concatenate([g[...] for g in gain_refs], axis=1)
            lane = lax.broadcasted_iota(jnp.int32, (rows, 128), 1)
            for i, block_ref in enumerate(block_refs):
                block = block_ref[...].astype(F32)
                x_ref[i * rows : (i + 1) * rows, :] = (block * gain).astype(BF)
                square = jnp.sum(block * block, axis=1, keepdims=True)
                high = square.astype(BF).astype(F32)
                middle = (square - high).astype(BF).astype(F32)
                low = square - high - middle
                out_ref[i, :, 2 * hidden :] = jnp.where(
                    lane == 0, high, jnp.where(lane == 1, middle, jnp.where(lane == 2, low, 0.0))
                ).astype(BF)

        for which, weights in enumerate((gate_refs, up_refs)):
            total = sum(
                jnp.dot(
                    x_ref[:, i * part : (i + 1) * part], w[...], preferred_element_type=F32
                )
                for i, w in enumerate(weights)
            )
            start = pl.multiple_of(which * hidden + step * tile, tile)
            out_ref[:, :, pl.ds(start, tile)] = total.astype(BF).reshape(count, rows, tile)

    weight_spec = pl.BlockSpec((part, tile), lambda j: (0, j))
    return pl.pallas_call(
        kernel,
        grid=(steps,),
        out_shape=jax.ShapeDtypeStruct((count, rows, full), BF),
        in_specs=[whole((rows, width))] * count + [whole((1, part))] * 2 + [weight_spec] * 4,
        out_specs=whole((count, rows, full)),
        scratch_shapes=[pltpu.VMEM((count * rows, width), BF)],
        compiler_params=params(),
        cost_estimate=cost(4 * count * rows * width * hidden, 12 * 10**6),
    )(*blocks, *gains, *gates, *ups)


def activate(parts, hidden, tile=256):
    count, rows, full = parts.shape
    steps = hidden // tile

    def kernel(gate_ref, up_ref, square_ref, out_ref, inv_ref):
        @pl.when(pl.program_id(0) == 0)
        def _():
            square = jnp.sum(square_ref[...].astype(F32), axis=(0, 2))[:, None]
            inv_ref[...] = jnp.broadcast_to(
                lax.rsqrt(square / MODEL_WIDTH + epsilon), inv_ref.shape
            )

        inverse = inv_ref[:, 0:1]
        gate = jnp.sum(gate_ref[...].astype(F32), axis=0) * inverse
        up = jnp.sum(up_ref[...].astype(F32), axis=0) * inverse
        value = (gate / (1.0 + jnp.exp(-gate)) * up).astype(BF)
        out_ref[...] = jnp.broadcast_to(value[None], out_ref.shape)

    return pl.pallas_call(
        kernel,
        grid=(steps,),
        out_shape=jax.ShapeDtypeStruct((CHIPS, rows, hidden), BF),
        in_specs=[
            pl.BlockSpec((count, rows, tile), lambda j: (0, 0, j)),
            pl.BlockSpec((count, rows, tile), lambda j: (0, 0, j + steps)),
            pl.BlockSpec((count, rows, 128), lambda j: (0, 0, 2 * hidden // 128)),
        ],
        out_specs=pl.BlockSpec((CHIPS, rows, tile), lambda j: (0, 0, j)),
        scratch_shapes=[pltpu.VMEM((rows, 128), F32)],
        compiler_params=params(),
        cost_estimate=cost(10**6, 6 * 10**6),
    )(parts, parts, parts)


def body(
    query,
    key_store_cache,
    value_store_cache,
    token_keys,
    token_values,
    pooled_block_keys,
    pooled_block_values,
    block_dst,
    block_row,
    ctx_len,
    residual,
    norm_gain,
    output_weight,
    w_gate,
    w_up,
    w_down,
):
    requests = query.shape[0]
    attn_index = lax.axis_index("attn")
    core = attn_index % 2
    ffn_index = lax.axis_index("ffn")
    pools = block_dst.shape[0] // pooled_block_keys.shape[0]
    flat_dst = block_dst[:, 0]

    output_far = swap_core(output_weight)
    first = ffn_index * (2 * requests)
    residual_near = lax.dynamic_slice_in_dim(residual, first + core * requests, requests, 0)
    residual_far = swap_core(
        lax.dynamic_slice_in_dim(residual, first + (1 - core) * requests, requests, 0)
    )
    gain_near = norm_gain.reshape(1, -1)
    gain_far = swap_core(gain_near)
    gate_far, up_far, down_far = swap_core(w_gate), swap_core(w_up), swap_core(w_down)

    sent = place_blocks(flat_dst, pooled_block_keys, pooled_block_values)
    received = lax.all_to_all(sent, "attn", split_axis=0, concat_axis=0, tiled=True)
    attended = attention(
        ctx_len,
        query,
        key_store_cache,
        value_store_cache,
        token_keys,
        token_values,
        received.reshape(-1, received.shape[2]),
        flat_dst.reshape(pools, -1),
        block_row.reshape(pools, -1),
    )
    attended = exchange_chips(attended).reshape(CHIPS * requests, -1)
    head_part = side_by_side(attended, output_weight, output_far).reshape(CHIPS, requests, -1)
    attn_out = z_scatter_sum(
        lambda d: lax.dynamic_index_in_dim(head_part, (ffn_index + d) % 8, 0, keepdims=False)
    )
    mixed = jnp.concatenate([residual_near, residual_far], axis=1).astype(F32) + attn_out
    blocks = z_gather(mixed.astype(BF))
    parts = gate_up(blocks, (gain_near, gain_far), (w_gate, gate_far), (w_up, up_far))
    activated = activate(exchange_chips(parts), w_gate.shape[1])
    activated = exchange_chips(activated).reshape(CHIPS * requests, -1)
    down_part = side_by_side(activated, w_down, down_far).reshape(CHIPS, requests, -1)
    ffn_out = z_scatter_sum(lambda d: down_part[d % 8])
    layer_out = (mixed + ffn_out).astype(BF)
    half = layer_out.shape[1] // 2
    near = layer_out[:, :half]
    far = swap_core(layer_out[:, half:])
    return jnp.where(
        core == 0, jnp.concatenate([near, far], axis=0), jnp.concatenate([far, near], axis=0)
    )


def solution(mesh):
    placed = (
        P(("grp", "attn"), "ffn"),
        P(("grp", "attn"), None, "ffn"),
        P(("grp", "attn"), None, "ffn"),
        P(("grp", "attn"), "ffn"),
        P(("grp", "attn"), "ffn"),
        P(("grp", "attn"), None, "ffn"),
        P(("grp", "attn"), None, "ffn"),
        P("grp", None),
        P("grp"),
        P(("grp", "attn")),
        P("grp", "attn"),
        P("attn"),
        P("ffn", "attn"),
        P("attn", "ffn"),
        P("attn", "ffn"),
        P("ffn", "attn"),
    )
    return jax.shard_map(
        body, mesh=mesh, in_specs=placed, out_specs=P(("grp", "ffn"), "attn"), check_vma=False
    )
```

```python
import jax
import jax.numpy as jnp
from jax import lax
from jax.experimental import pallas as pl
from jax.experimental.pallas import tpu as pltpu
from jax.sharding import PartitionSpec as P

MODEL_WIDTH = 8192
HEAD_SIZE = 128
HEADS = 8
CAP = 2
epsilon = 1e-05
BF = jnp.bfloat16
F32 = jnp.float32
NT = (((1,), (1,)), ((), ()))


def params(mebibytes=40):
    return pltpu.CompilerParams(vmem_limit_bytes=mebibytes * 1024 * 1024)


def whole(shape):
    return pl.BlockSpec(shape, lambda *_: (0,) * len(shape))


def cost(flops, size):
    return pl.CostEstimate(flops=flops, bytes_accessed=size, transcendentals=0)


def swap(value, bits):
    return lax.ppermute(value, "attn", [(a, a ^ bits) for a in range(16)])


def exchange_chips(value):
    groups = [[2 * k + c for k in range(8)] for c in range(2)]
    return lax.all_to_all(
        value, "attn", split_axis=0, concat_axis=0, axis_index_groups=groups, tiled=True
    )


def chip_gather(value):
    blocks = [value]
    for i in range(1, 8):
        pairs = [(a, (a & 1) | ((((a >> 1) - i) & 3) << 1) | ((a & 8) ^ (i // 4 * 8))) for a in range(16)]
        blocks.append(lax.ppermute(value, "attn", pairs))
    return blocks


def gathered_at(chip):
    own = lax.shift_right_logical(lax.axis_index("attn"), 1)
    return ((chip ^ own) & 4) | ((chip - own) & 3)


def together(*values):
    return lax.optimization_barrier(values)


def z_shift(value, step):
    return lax.ppermute(value, "ffn", [(f, (f + step) % 8) for f in range(8)])


def added(moved, block):
    return (moved.astype(F32) + block.astype(F32)).astype(BF)


def z_scatter_sum(blocks):
    rows = blocks[0].shape[0] // 2
    first = (
        z_shift(blocks[4][:rows], 2),
        z_shift(blocks[4][rows:], -2),
        z_shift(blocks[3], 1),
        z_shift(blocks[5], -1),
    )
    top, bottom, from_left, from_right, *beside = together(*first, blocks[1], blocks[7])
    right = added(from_left, blocks[2])
    right = jnp.concatenate([added(top, right[:rows]), right[rows:]], axis=0)
    left = added(from_right, blocks[6])
    left = jnp.concatenate([left[:rows], added(bottom, left[rows:])], axis=0)
    return (
        z_shift(right, 2),
        z_shift(left, -2),
        z_shift(beside[0], 1),
        z_shift(beside[1], -1),
        blocks[0],
    )


def z_gather(value):
    rows = value.shape[0] // 2
    right, left, *beside = together(
        z_shift(value, 2), z_shift(value, -2), z_shift(value, 1), z_shift(value, -1)
    )
    top, bottom = z_shift(left[:rows], -2), z_shift(right[rows:], 2)
    far = z_shift(right, 1), z_shift(left, -1)
    return [value, beside[1], left, far[1], top, bottom, far[0], right, beside[0]]


def place_blocks(block_dst, pooled_keys, pooled_values, residual, norm_gain, kept):
    held, block_len, width = pooled_keys.shape
    slots = 16 * CAP
    columns = residual.shape[1]

    def kernel(dst_ref, k_ref, v_ref, gain_ref, res_ref, out_ref, *rest):
        piece_refs, buf, sems = rest[:2], rest[2], rest[3]
        index = lax.axis_index("attn")
        ffn_index = lax.axis_index("ffn")
        copies = []
        for i in range(2):
            start = pl.multiple_of((2 * ffn_index + ((index & 1) ^ i)) * kept, kept)
            copies.append(
                pltpu.make_async_copy(res_ref.at[pl.ds(start, kept)], buf.at[i], sems.at[i])
            )
            copies[i].start()
        first = index * held
        out_ref[...] = jnp.zeros_like(out_ref)
        dst = [dst_ref[first + j] for j in range(held)]
        for j in range(held):
            rank = jnp.int32(0)
            for i in range(j):
                rank = rank + jnp.where(dst[i] == dst[j], 1, 0)
            slot = dst[j] * CAP + jnp.minimum(rank, CAP - 1)
            out_ref[slot, :, :width] = k_ref[j]
            out_ref[slot, :, width:] = v_ref[j]
        gain = gain_ref[...]
        high = gain.astype(BF).astype(F32)
        middle = (gain - high).astype(BF).astype(F32)
        low = gain - high - middle
        row = lax.broadcasted_iota(jnp.int32, (16, columns), 0)
        gain_rows = jnp.where(
            row == 0, high, jnp.where(row == 1, middle, jnp.where(row == 2, low, 0.0))
        ).astype(BF)
        for i in range(2):
            copies[i].wait()
            piece_refs[i][:kept, :] = buf[i]
            piece_refs[i][kept:, :] = gain_rows

    return pl.pallas_call(
        kernel,
        out_shape=[jax.ShapeDtypeStruct((slots, block_len, 2 * width), BF)]
        + [jax.ShapeDtypeStruct((kept + 16, columns), BF)] * 2,
        in_specs=[
            pl.BlockSpec(memory_space=pltpu.SMEM),
            pl.BlockSpec(memory_space=pltpu.VMEM),
            pl.BlockSpec(memory_space=pltpu.VMEM),
            pl.BlockSpec(memory_space=pltpu.VMEM),
            pl.BlockSpec(memory_space=pltpu.HBM),
        ],
        out_specs=[pl.BlockSpec(memory_space=pltpu.VMEM)] * 3,
        scratch_shapes=[
            pltpu.VMEM((2, kept, columns), BF),
            pltpu.SemaphoreType.DMA((2,)),
        ],
        compiler_params=params(62),
    )(block_dst, pooled_keys, pooled_values, norm_gain.reshape(1, -1), residual)


def spread_heads(source_ref, target, count):
    for h in range(HEADS):
        target[pl.ds(h, count, stride=HEADS), :] = source_ref[
            :, h * HEAD_SIZE : (h + 1) * HEAD_SIZE
        ].astype(F32)


def cached_attention(ctx_len, query, keys, values, token_keys, token_values):
    requests, ctx_size, width = keys.shape
    step_rows = 16
    scale = HEAD_SIZE**-0.5
    hrows = step_rows * HEADS

    def kernel(
        ctx_ref, q_ref, k_ref, v_ref, tk_ref, tv_ref, out_ref, stat_ref, q_buf, tk_buf, tv_buf
    ):
        step = pl.program_id(0)
        spread_heads(q_ref, q_buf, step_rows)
        for h in range(HEADS):
            tk_buf[pl.ds(h, step_rows, stride=HEADS), :] = tk_ref[...].astype(F32)
            tv_buf[pl.ds(h, step_rows, stride=HEADS), :] = tv_ref[...].astype(F32)
        q_full = q_buf[...]
        q_half = q_full.astype(BF)
        scores = []
        spot = lax.broadcasted_iota(jnp.int32, (HEADS, ctx_size), 1)
        for b in range(step_rows):
            part = lax.dot_general(
                q_half[b * HEADS : (b + 1) * HEADS], k_ref[b], NT, preferred_element_type=F32
            )
            scores.append(
                jnp.where(spot < ctx_ref[step * step_rows + b], part * scale, -jnp.inf)
            )
        score_cache = jnp.concatenate(scores, axis=0)
        score_new = jnp.sum(q_full * tk_buf[...], axis=1, keepdims=True) * scale
        top = jnp.maximum(jnp.max(score_cache, axis=1, keepdims=True), score_new)
        exp_cache = jnp.exp(score_cache - top)
        exp_new = jnp.exp(score_new - top)
        total = jnp.sum(exp_cache, axis=1, keepdims=True) + exp_new
        prob_cache = exp_cache.astype(BF)
        prob_new = exp_new.astype(BF).astype(F32)
        attended = [
            jnp.dot(
                prob_cache[b * HEADS : (b + 1) * HEADS], v_ref[b], preferred_element_type=F32
            )
            for b in range(step_rows)
        ]
        out_ref[...] = jnp.concatenate(attended, axis=0) + prob_new * tv_buf[...]
        lane = lax.broadcasted_iota(jnp.int32, stat_ref.shape, 1)
        stat_ref[...] = jnp.where(lane < width // 2, top, total)

    result = jax.ShapeDtypeStruct((requests * HEADS, width), F32)
    return pl.pallas_call(
        kernel,
        grid=(requests // step_rows,),
        out_shape=(result,) * 2,
        in_specs=[
            pl.BlockSpec(memory_space=pltpu.SMEM),
            pl.BlockSpec((step_rows, query.shape[1]), lambda i: (i, 0)),
            pl.BlockSpec((step_rows, ctx_size, width), lambda i: (i, 0, 0)),
            pl.BlockSpec((step_rows, ctx_size, width), lambda i: (i, 0, 0)),
            pl.BlockSpec((step_rows, width), lambda i: (i, 0)),
            pl.BlockSpec((step_rows, width), lambda i: (i, 0)),
        ],
        out_specs=(pl.BlockSpec((hrows, width), lambda i: (i, 0)),) * 2,
        scratch_shapes=[pltpu.VMEM((hrows, HEAD_SIZE), F32)] * 3,
        compiler_params=params(62),
        cost_estimate=cost(10**8, 7 * 10**6),
    )(ctx_len, query, keys, values, token_keys, token_values)


def merge_received(query, cached, stats, received, dst, rows):
    requests = query.shape[0]
    width = cached.shape[1]
    step_rows = 16
    slots = 16 * CAP
    recv_size = received.shape[0]
    block_len = recv_size // slots
    scale = HEAD_SIZE**-0.5
    hrows = step_rows * HEADS

    def kernel(
        q_ref, part_ref, stat_ref, r_ref, dst_ref, row_ref, out_ref, owner_ref, q_buf, o_buf
    ):
        step = pl.program_id(0)

        @pl.when(step == 0)
        def _():
            count = dst_ref.shape[1]
            held = 2 * count // slots
            hit = (dst_ref[...] == lax.axis_index("attn")).astype(F32)
            source = lax.broadcasted_iota(jnp.int32, (count, count), 0)
            target = lax.broadcasted_iota(jnp.int32, (count, count), 1)
            earlier = (source < target) & (source // held == target // held)
            rank = jnp.dot(
                jnp.broadcast_to(hit, (8, count)), earlier.astype(F32), preferred_element_type=F32
            )
            marked = hit * (row_ref[...].astype(F32) + 1.0)
            pool = lax.broadcasted_iota(jnp.int32, (count, recv_size), 0) // held
            slot = lax.broadcasted_iota(jnp.int32, (count, recv_size), 1) // block_len
            owner = jnp.full(owner_ref.shape, -1.0, F32)
            for i in range(CAP):
                chosen = jnp.where(jnp.abs(rank - i) < 0.5, marked, 0.0)
                owner = owner + jnp.dot(
                    chosen, (slot == pool * CAP + i).astype(F32), preferred_element_type=F32
                )
            owner_ref[...] = owner

        spread_heads(q_ref, q_buf, step_rows)
        score = (
            lax.dot_general(
                q_buf[...].astype(BF), r_ref[:, :width], NT, preferred_element_type=F32
            )
            * scale
        )
        request = (
            lax.broadcasted_iota(jnp.int32, (hrows, recv_size), 0) // HEADS + step * step_rows
        )
        score = jnp.where(request.astype(F32) == owner_ref[0:1, :], score, -jnp.inf)
        cached_top = stat_ref[:, 0:1]
        top = jnp.maximum(cached_top, jnp.max(score, axis=1, keepdims=True))
        exp_recv = jnp.exp(score - top)
        shrink = jnp.exp(cached_top - top)
        total = stat_ref[:, width - 1 : width] * shrink + jnp.sum(exp_recv, axis=1, keepdims=True)
        o_buf[...] = (
            part_ref[...] * shrink
            + jnp.dot(exp_recv.astype(BF), r_ref[:, width:], preferred_element_type=F32)
        ) / total
        for h in range(HEADS):
            head = o_buf[pl.ds(h, step_rows, stride=HEADS), :].astype(BF)
            out_ref[:, h * HEAD_SIZE : (h + 1) * HEAD_SIZE] = head

    part_spec = pl.BlockSpec((hrows, width), lambda i: (i, 0))
    return pl.pallas_call(
        kernel,
        grid=(requests // step_rows,),
        out_shape=jax.ShapeDtypeStruct((requests, query.shape[1]), BF),
        in_specs=[
            pl.BlockSpec((step_rows, query.shape[1]), lambda i: (i, 0)),
            part_spec,
            part_spec,
            whole(received.shape),
            whole(dst.shape),
            whole(rows.shape),
        ],
        out_specs=pl.BlockSpec((step_rows, query.shape[1]), lambda i: (i, 0)),
        scratch_shapes=[
            pltpu.VMEM((8, recv_size), F32),
            pltpu.VMEM((hrows, HEAD_SIZE), F32),
            pltpu.VMEM((hrows, HEAD_SIZE), F32),
        ],
        compiler_params=params(24),
        cost_estimate=cost(10**8, 3 * 10**6),
    )(query, cached, stats, received, dst, rows)


def fetch(sources, targets, sems):
    copies = [
        pltpu.make_async_copy(source, target, sems.at[i])
        for i, (source, target) in enumerate(zip(sources, targets, strict=True))
    ]
    for copy in copies:
        copy.start()
    return copies


def side_by_side(x_blocks, weights, first, tile=256):
    rows, k = x_blocks[0].shape
    m = rows * len(x_blocks)
    n = weights[0].shape[1]
    count = len(weights)

    def kernel(*refs):
        block_refs, refs = refs[: len(x_blocks)], refs[len(x_blocks) :]
        weight_refs, refs = refs[:count], refs[count:]
        out_ref, x_ref, *held, sems = refs
        copies = fetch(weight_refs, held, sems)
        start = first()
        for d in range(8):
            index = gathered_at((start + d) & 7)
            for i, block_ref in enumerate(block_refs):

                @pl.when(index == i)
                def _(d=d, block_ref=block_ref):
                    x_ref[d * rows : (d + 1) * rows, :] = block_ref[...]

        for i, copy in enumerate(copies):
            copy.wait()
            for j in range(n // tile):
                out_ref[:, :, i * n + j * tile : i * n + (j + 1) * tile] = (
                    jnp.dot(
                        x_ref[...],
                        held[i][:, j * tile : (j + 1) * tile],
                        preferred_element_type=F32,
                    )
                    .astype(BF)
                    .reshape(8, rows, tile)
                )

    return pl.pallas_call(
        kernel,
        out_shape=jax.ShapeDtypeStruct((8, rows, count * n), BF),
        in_specs=[pl.BlockSpec(memory_space=pltpu.VMEM)] * len(x_blocks)
        + [pl.BlockSpec(memory_space=pltpu.HBM)] * count,
        out_specs=pl.BlockSpec(memory_space=pltpu.VMEM),
        scratch_shapes=[pltpu.VMEM((m, k), BF)]
        + [pltpu.VMEM((k, n), BF)] * count
        + [pltpu.SemaphoreType.DMA((count,))],
        compiler_params=params(),
        cost_estimate=cost(2 * m * count * n * k, 2 * (m * k + k * n * count + m * n * count)),
    )(*x_blocks, *weights)


def settle(terms, extras):
    kept, width = terms[0].shape
    part = width // len(extras)

    def kernel(*refs):
        term_refs, refs = refs[: len(terms)], refs[len(terms) :]
        extra_refs, (mixed_ref, half_ref) = refs[: len(extras)], refs[len(extras) :]
        for i, extra_ref in enumerate(extra_refs):
            columns = slice(i * part, (i + 1) * part)
            total = sum(t[:, columns].astype(F32) for t in term_refs)
            total = total + extra_ref[:kept, :].astype(F32)
            mixed_ref[:, columns] = total
            half_ref[:, columns] = total.astype(BF)

    return pl.pallas_call(
        kernel,
        out_shape=(
            jax.ShapeDtypeStruct((kept, width), F32),
            jax.ShapeDtypeStruct((kept, width), BF),
        ),
        compiler_params=params(),
    )(*terms, *extras)


def gate_up(blocks, extras, gates, ups, tile=256):
    count = len(blocks)
    width = blocks[0].shape[1]
    rows = sum(block.shape[0] for block in blocks)
    pieces = len(gates)
    part = width // pieces
    hidden = gates[0].shape[1]
    kept = extras[0].shape[0] - 16

    def kernel(*refs):
        block_refs, refs = refs[:count], refs[count:]
        extra_refs, refs = refs[:pieces], refs[pieces:]
        weight_refs, (out_ref, x_ref) = refs[: 2 * pieces], refs[2 * pieces :]
        gain = jnp.concatenate(
            [
                jnp.sum(e[...].astype(F32)[kept : kept + 3], axis=0, keepdims=True)
                for e in extra_refs
            ],
            axis=1,
        )
        start = 0
        for block_ref in block_refs:
            size = block_ref.shape[0]
            spot = slice(start, start + size)
            block = block_ref[...].astype(F32)
            x_ref[spot, :] = (block * gain).astype(BF)
            square = jnp.sum(block * block, axis=1, keepdims=True)
            high = square.astype(BF).astype(F32)
            middle = (square - high).astype(BF).astype(F32)
            low = square - high - middle
            lane = lax.broadcasted_iota(jnp.int32, (size, 128), 1)
            out_ref[spot, 2 * hidden :] = jnp.where(
                lane == 0, high, jnp.where(lane == 1, middle, jnp.where(lane == 2, low, 0.0))
            ).astype(BF)
            start += size
        for which in range(2):
            for j in range(hidden // tile):
                out_ref[:, which * hidden + j * tile : which * hidden + (j + 1) * tile] = sum(
                    jnp.dot(
                        x_ref[:, i * part : (i + 1) * part],
                        weight_refs[which * pieces + i][:, j * tile : (j + 1) * tile],
                        preferred_element_type=F32,
                    )
                    for i in range(pieces)
                ).astype(BF)

    return pl.pallas_call(
        kernel,
        out_shape=jax.ShapeDtypeStruct((rows, 2 * hidden + 128), BF),
        scratch_shapes=[pltpu.VMEM((rows, width), BF)],
        compiler_params=params(24),
        cost_estimate=cost(4 * rows * width * hidden, 4 * width * hidden),
    )(*blocks, *extras, *gates, *ups)


def activate(parts, hidden, tile=896):
    count, rows, _ = parts.shape
    steps = hidden // tile

    def kernel(gate_ref, up_ref, square_ref, out_ref, inv_ref):
        @pl.when(pl.program_id(0) == 0)
        def _():
            square = jnp.sum(square_ref[...].astype(F32), axis=(0, 2))[:, None]
            inv_ref[...] = jnp.broadcast_to(
                lax.rsqrt(square / MODEL_WIDTH + epsilon), inv_ref.shape
            )

        inverse = inv_ref[:, 0:1]
        gate = jnp.sum(gate_ref[...].astype(F32), axis=0) * inverse
        up = jnp.sum(up_ref[...].astype(F32), axis=0) * inverse
        out_ref[...] = (gate / (1.0 + jnp.exp(-gate)) * up).astype(BF)

    return pl.pallas_call(
        kernel,
        grid=(steps,),
        out_shape=jax.ShapeDtypeStruct((rows, hidden), BF),
        in_specs=[
            pl.BlockSpec((count, rows, tile), lambda j: (0, 0, j)),
            pl.BlockSpec((count, rows, tile), lambda j: (0, 0, j + steps)),
            pl.BlockSpec((count, rows, 128), lambda j: (0, 0, 2 * hidden // 128)),
        ],
        out_specs=pl.BlockSpec((rows, tile), lambda j: (0, j)),
        scratch_shapes=[pltpu.VMEM((rows, 128), F32)],
        compiler_params=params(),
        cost_estimate=cost(10**6, 6 * 10**6),
    )(parts, parts, parts)


def body(
    query,
    key_store_cache,
    value_store_cache,
    token_keys,
    token_values,
    pooled_block_keys,
    pooled_block_values,
    block_dst,
    block_row,
    ctx_len,
    residual,
    norm_gain,
    output_weight,
    w_gate,
    w_up,
    w_down,
):
    requests = query.shape[0]
    core = lax.axis_index("attn") & 1
    flat_dst = block_dst[:, 0]

    sent, piece, piece_far = place_blocks(
        flat_dst, pooled_block_keys, pooled_block_values, residual, norm_gain, requests
    )
    received = lax.all_to_all(sent, "attn", split_axis=0, concat_axis=0, tiled=True)
    cached = cached_attention(
        ctx_len, query, key_store_cache, value_store_cache, token_keys, token_values
    )
    extras = [piece, swap(piece_far, 1)]
    weights = output_weight, w_gate, w_up, w_down
    fars = [swap(w, 1) for w in weights]
    received, *late = together(received, *cached, *fars, *extras)
    cached, fars, extras = late[:2], late[2:6], late[6:]

    attended = merge_received(
        query,
        *cached,
        received.reshape(-1, received.shape[2]),
        flat_dst.reshape(1, -1),
        block_row.reshape(1, -1),
    )
    head_part = side_by_side(
        chip_gather(attended), (output_weight, fars[0]), lambda: lax.axis_index("ffn")
    )
    mixed, half_mixed = settle(z_scatter_sum(head_part), extras)
    parts = gate_up(z_gather(half_mixed), extras, (w_gate, fars[1]), (w_up, fars[2]))
    parts = exchange_chips(parts.reshape(8, requests, -1))
    activated = chip_gather(activate(parts, w_gate.shape[1]))
    terms = z_scatter_sum(side_by_side(activated, (w_down, fars[3]), lambda: 0))

    layer_out = (mixed + sum(t.astype(F32) for t in terms)).astype(BF)
    half = layer_out.shape[1] // 2
    near = layer_out[:, :half]
    far = swap(layer_out[:, half:], 1)
    return jnp.where(
        core == 0, jnp.concatenate([near, far], axis=0), jnp.concatenate([far, near], axis=0)
    )


def solution(mesh):
    placed = (
        P(("grp", "attn"), "ffn"),
        P(("grp", "attn"), None, "ffn"),
        P(("grp", "attn"), None, "ffn"),
        P(("grp", "attn"), "ffn"),
        P(("grp", "attn"), "ffn"),
        P(("grp", "attn"), None, "ffn"),
        P(("grp", "attn"), None, "ffn"),
        P("grp", None),
        P("grp"),
        P(("grp", "attn")),
        P("grp", "attn"),
        P("attn"),
        P("ffn", "attn"),
        P("attn", "ffn"),
        P("attn", "ffn"),
        P("ffn", "attn"),
    )
    return jax.shard_map(
        body, mesh=mesh, in_specs=placed, out_specs=P(("grp", "ffn"), "attn"), check_vma=False
    )
```

```python
import jax
import jax.numpy as jnp
from jax import lax
from jax.experimental import pallas as pl
from jax.experimental.pallas import tpu as pltpu
from jax.sharding import PartitionSpec as P

MODEL_WIDTH = 8192
HEAD_SIZE = 128
HEADS = 8
CAP = 2
epsilon = 1e-05
BF = jnp.bfloat16
F32 = jnp.float32
NT = (((1,), (1,)), ((), ()))


def params(mebibytes=40):
    return pltpu.CompilerParams(vmem_limit_bytes=mebibytes * 1024 * 1024)


def whole(shape):
    return pl.BlockSpec(shape, lambda *_: (0,) * len(shape))


def cost(flops, size):
    return pl.CostEstimate(flops=flops, bytes_accessed=size, transcendentals=0)


def swap(value, bits):
    return lax.ppermute(value, "attn", [(a, a ^ bits) for a in range(16)])


def x_scatter(blocks):
    moved = [blocks[0]]
    for i in range(1, 4):
        pairs = [(a, (a & 9) | ((((a >> 1) + i) & 3) << 1)) for a in range(16)]
        moved.append(lax.ppermute(blocks[i], "attn", pairs))
    return moved


def chip_gather(value):
    blocks = []
    other = swap(value, 8)
    for start in (value, other):
        blocks.append(start)
        for step in range(1, 4):
            pairs = [(a, (a & 9) | ((((a >> 1) - step) & 3) << 1)) for a in range(16)]
            blocks.append(lax.ppermute(start, "attn", pairs))
    return blocks


def distance_to(chip):
    own = lax.shift_right_logical(lax.axis_index("attn"), 1)
    return ((chip ^ own) & 4) | ((chip - own) & 3)


def together(*values):
    return lax.optimization_barrier(values)


def z_shift(value, step):
    return lax.ppermute(value, "ffn", [(f, (f + step) % 8) for f in range(8)])


def added(moved, block):
    return (moved.astype(F32) + block.astype(F32)).astype(BF)


def z_scatter_sum(blocks, beside_last):
    rows = blocks[0].shape[0] // 2
    first = (
        z_shift(blocks[4][:rows], 2),
        z_shift(blocks[4][rows:], -2),
        z_shift(blocks[3], 1),
        z_shift(blocks[5], -1),
    )
    beside = blocks[1], blocks[7]
    if beside_last:
        *first, beside_right, beside_left = together(*first, *beside)
        beside = beside_right, beside_left
    top, bottom, from_left, from_right = first
    right = added(from_left, blocks[2])
    right = jnp.concatenate([added(top, right[:rows]), right[rows:]], axis=0)
    left = added(from_right, blocks[6])
    left = jnp.concatenate([left[:rows], added(bottom, left[rows:])], axis=0)
    return (
        z_shift(right, 2),
        z_shift(left, -2),
        z_shift(beside[0], 1),
        z_shift(beside[1], -1),
        blocks[0],
    )


def z_gather(value):
    rows = value.shape[0] // 2
    right, left, *beside = together(
        z_shift(value, 2), z_shift(value, -2), z_shift(value, 1), z_shift(value, -1)
    )
    top, bottom = z_shift(left[:rows], -2), z_shift(right[rows:], 2)
    far = z_shift(right, 1), z_shift(left, -1)
    return [value, beside[1], left, far[1], top, bottom, far[0], right, beside[0]]


def place_blocks(block_dst, pooled_keys, pooled_values, residual, norm_gain, kept):
    held, block_len, width = pooled_keys.shape
    slots = 16 * CAP
    columns = residual.shape[1]

    def kernel(dst_ref, k_ref, v_ref, gain_ref, res_ref, out_ref, *rest):
        piece_refs, buf, sems = rest[:2], rest[2], rest[3]
        index = lax.axis_index("attn")
        ffn_index = lax.axis_index("ffn")
        copies = []
        for i in range(2):
            start = pl.multiple_of((2 * ffn_index + ((index & 1) ^ i)) * kept, kept)
            copies.append(
                pltpu.make_async_copy(res_ref.at[pl.ds(start, kept)], buf.at[i], sems.at[i])
            )
            copies[i].start()
        first = index * held
        out_ref[...] = jnp.zeros_like(out_ref)
        dst = [dst_ref[first + j] for j in range(held)]
        for j in range(held):
            rank = jnp.int32(0)
            for i in range(j):
                rank = rank + jnp.where(dst[i] == dst[j], 1, 0)
            slot = dst[j] * CAP + jnp.minimum(rank, CAP - 1)
            out_ref[slot, :, :width] = k_ref[j]
            out_ref[slot, :, width:] = v_ref[j]
        gain = gain_ref[...]
        high = gain.astype(BF).astype(F32)
        middle = (gain - high).astype(BF).astype(F32)
        low = gain - high - middle
        row = lax.broadcasted_iota(jnp.int32, (16, columns), 0)
        gain_rows = jnp.where(
            row == 0, high, jnp.where(row == 1, middle, jnp.where(row == 2, low, 0.0))
        ).astype(BF)
        for i in range(2):
            copies[i].wait()
            piece_refs[i][:kept, :] = buf[i]
            piece_refs[i][kept:, :] = gain_rows

    return pl.pallas_call(
        kernel,
        out_shape=[jax.ShapeDtypeStruct((slots, block_len, 2 * width), BF)]
        + [jax.ShapeDtypeStruct((kept + 16, columns), BF)] * 2,
        in_specs=[
            pl.BlockSpec(memory_space=pltpu.SMEM),
            pl.BlockSpec(memory_space=pltpu.VMEM),
            pl.BlockSpec(memory_space=pltpu.VMEM),
            pl.BlockSpec(memory_space=pltpu.VMEM),
            pl.BlockSpec(memory_space=pltpu.HBM),
        ],
        out_specs=[pl.BlockSpec(memory_space=pltpu.VMEM)] * 3,
        scratch_shapes=[
            pltpu.VMEM((2, kept, columns), BF),
            pltpu.SemaphoreType.DMA((2,)),
        ],
        compiler_params=params(62),
    )(block_dst, pooled_keys, pooled_values, norm_gain.reshape(1, -1), residual)


def spread_heads(source_ref, target, count):
    for h in range(HEADS):
        target[pl.ds(h, count, stride=HEADS), :] = source_ref[
            :, h * HEAD_SIZE : (h + 1) * HEAD_SIZE
        ].astype(F32)


def cached_attention(ctx_len, query, keys, values, token_keys, token_values):
    requests, ctx_size, width = keys.shape
    step_rows = 16
    scale = HEAD_SIZE**-0.5
    hrows = step_rows * HEADS

    def kernel(
        ctx_ref, q_ref, k_ref, v_ref, tk_ref, tv_ref, out_ref, q_buf, tk_buf, tv_buf
    ):
        step = pl.program_id(0)
        spread_heads(q_ref, q_buf, step_rows)
        for h in range(HEADS):
            tk_buf[pl.ds(h, step_rows, stride=HEADS), :] = tk_ref[...].astype(F32)
            tv_buf[pl.ds(h, step_rows, stride=HEADS), :] = tv_ref[...].astype(F32)
        q_full = q_buf[...]
        q_half = q_full.astype(BF)
        scores = []
        spot = lax.broadcasted_iota(jnp.int32, (HEADS, ctx_size), 1)
        for b in range(step_rows):
            part = lax.dot_general(
                q_half[b * HEADS : (b + 1) * HEADS], k_ref[b], NT, preferred_element_type=F32
            )
            scores.append(
                jnp.where(spot < ctx_ref[step * step_rows + b], part * scale, -jnp.inf)
            )
        score_cache = jnp.concatenate(scores, axis=0)
        score_new = jnp.sum(q_full * tk_buf[...], axis=1, keepdims=True) * scale
        top = jnp.maximum(jnp.max(score_cache, axis=1, keepdims=True), score_new)
        exp_cache = jnp.exp(score_cache - top)
        exp_new = jnp.exp(score_new - top)
        total = jnp.sum(exp_cache, axis=1, keepdims=True) + exp_new
        prob_cache = exp_cache.astype(BF)
        prob_new = exp_new.astype(BF).astype(F32)
        attended = [
            jnp.dot(
                prob_cache[b * HEADS : (b + 1) * HEADS], v_ref[b], preferred_element_type=F32
            )
            for b in range(step_rows)
        ]
        out_ref[:, :width] = jnp.concatenate(attended, axis=0) + prob_new * tv_buf[...]
        lane = lax.broadcasted_iota(jnp.int32, (hrows, width), 1)
        out_ref[:, width:] = jnp.where(lane < width // 2, top, total)

    return pl.pallas_call(
        kernel,
        grid=(requests // step_rows,),
        out_shape=jax.ShapeDtypeStruct((requests * HEADS, 2 * width), F32),
        in_specs=[
            pl.BlockSpec(memory_space=pltpu.SMEM),
            pl.BlockSpec((step_rows, query.shape[1]), lambda i: (i, 0)),
            pl.BlockSpec((step_rows, ctx_size, width), lambda i: (i, 0, 0)),
            pl.BlockSpec((step_rows, ctx_size, width), lambda i: (i, 0, 0)),
            pl.BlockSpec((step_rows, width), lambda i: (i, 0)),
            pl.BlockSpec((step_rows, width), lambda i: (i, 0)),
        ],
        out_specs=pl.BlockSpec((hrows, 2 * width), lambda i: (i, 0)),
        scratch_shapes=[pltpu.VMEM((hrows, HEAD_SIZE), F32)] * 3,
        compiler_params=params(56),
        cost_estimate=cost(10**8, 7 * 10**6),
    )(ctx_len, query, keys, values, token_keys, token_values)


def merge_received(query, cached, received, dst, rows):
    requests = query.shape[0]
    width = cached.shape[1] // 2
    step_rows = 16
    slots = 16 * CAP
    recv_size = received.shape[0]
    block_len = recv_size // slots
    scale = HEAD_SIZE**-0.5
    hrows = step_rows * HEADS

    def kernel(
        q_ref, part_ref, r_ref, dst_ref, row_ref, out_ref, owner_ref, q_buf, o_buf
    ):
        step = pl.program_id(0)

        @pl.when(step == 0)
        def _():
            count = dst_ref.shape[1]
            held = 2 * count // slots
            hit = (dst_ref[...] == lax.axis_index("attn")).astype(F32)
            source = lax.broadcasted_iota(jnp.int32, (count, count), 0)
            target = lax.broadcasted_iota(jnp.int32, (count, count), 1)
            earlier = (source < target) & (source // held == target // held)
            rank = jnp.dot(
                jnp.broadcast_to(hit, (8, count)), earlier.astype(F32), preferred_element_type=F32
            )
            marked = hit * (row_ref[...].astype(F32) + 1.0)
            pool = lax.broadcasted_iota(jnp.int32, (count, recv_size), 0) // held
            slot = lax.broadcasted_iota(jnp.int32, (count, recv_size), 1) // block_len
            owner = jnp.full(owner_ref.shape, -1.0, F32)
            for i in range(CAP):
                chosen = jnp.where(jnp.abs(rank - i) < 0.5, marked, 0.0)
                owner = owner + jnp.dot(
                    chosen, (slot == pool * CAP + i).astype(F32), preferred_element_type=F32
                )
            owner_ref[...] = owner

        spread_heads(q_ref, q_buf, step_rows)
        score = (
            lax.dot_general(
                q_buf[...].astype(BF), r_ref[:, :width], NT, preferred_element_type=F32
            )
            * scale
        )
        request = (
            lax.broadcasted_iota(jnp.int32, (hrows, recv_size), 0) // HEADS + step * step_rows
        )
        score = jnp.where(request.astype(F32) == owner_ref[0:1, :], score, -jnp.inf)
        cached_top = part_ref[:, width : width + 1]
        top = jnp.maximum(cached_top, jnp.max(score, axis=1, keepdims=True))
        exp_recv = jnp.exp(score - top)
        shrink = jnp.exp(cached_top - top)
        total = part_ref[:, 2 * width - 1 :] * shrink + jnp.sum(exp_recv, axis=1, keepdims=True)
        o_buf[...] = (
            part_ref[:, :width] * shrink
            + jnp.dot(exp_recv.astype(BF), r_ref[:, width:], preferred_element_type=F32)
        ) / total
        for h in range(HEADS):
            head = o_buf[pl.ds(h, step_rows, stride=HEADS), :].astype(BF)
            out_ref[:, h * HEAD_SIZE : (h + 1) * HEAD_SIZE] = head

    part_spec = pl.BlockSpec((hrows, 2 * width), lambda i: (i, 0))
    return pl.pallas_call(
        kernel,
        grid=(requests // step_rows,),
        out_shape=jax.ShapeDtypeStruct((requests, query.shape[1]), BF),
        in_specs=[
            pl.BlockSpec((step_rows, query.shape[1]), lambda i: (i, 0)),
            part_spec,
            whole(received.shape),
            whole(dst.shape),
            whole(rows.shape),
        ],
        out_specs=pl.BlockSpec((step_rows, query.shape[1]), lambda i: (i, 0)),
        scratch_shapes=[
            pltpu.VMEM((8, recv_size), F32),
            pltpu.VMEM((hrows, HEAD_SIZE), F32),
            pltpu.VMEM((hrows, HEAD_SIZE), F32),
        ],
        compiler_params=params(24),
        cost_estimate=cost(10**8, 3 * 10**6),
    )(query, cached, received, dst, rows)


def side_by_side(x_blocks, weights, first, wanted, tile=256):
    rows, k = x_blocks[0].shape
    m = rows * len(wanted)
    n = weights[0].shape[1]
    count = len(weights)

    def kernel(*refs):
        block_refs, refs = refs[: len(x_blocks)], refs[len(x_blocks) :]
        weight_refs, (out_ref, x_ref) = refs[:count], refs[count:]
        start = first()
        for p, d in enumerate(wanted):
            index = distance_to((start + d) & 7)
            for i, block_ref in enumerate(block_refs):

                @pl.when(index == i)
                def _(p=p, block_ref=block_ref):
                    x_ref[p * rows : (p + 1) * rows, :] = block_ref[...]

        for i, weight_ref in enumerate(weight_refs):
            for j in range(n // tile):
                out_ref[:, :, i * n + j * tile : i * n + (j + 1) * tile] = (
                    jnp.dot(
                        x_ref[...],
                        weight_ref[:, j * tile : (j + 1) * tile],
                        preferred_element_type=F32,
                    )
                    .astype(BF)
                    .reshape(len(wanted), rows, tile)
                )

    return pl.pallas_call(
        kernel,
        out_shape=jax.ShapeDtypeStruct((len(wanted), rows, count * n), BF),
        scratch_shapes=[pltpu.VMEM((m, k), BF)],
        compiler_params=params(24),
        cost_estimate=cost(2 * m * count * n * k, 2 * (m * k + k * n * count + m * n * count)),
    )(*x_blocks, *weights)


def product_sum(x_blocks, weights, first, beside_last):
    far = side_by_side(x_blocks, weights, first, (3, 4, 5))
    near = side_by_side(x_blocks, weights, first, (0, 1, 2, 6, 7))
    return z_scatter_sum([*near[:3], *far, *near[3:]], beside_last)


def settle(terms, extras):
    kept, width = terms[0].shape
    part = width // len(extras)

    def kernel(*refs):
        term_refs, refs = refs[: len(terms)], refs[len(terms) :]
        extra_refs, (mixed_ref, half_ref) = refs[: len(extras)], refs[len(extras) :]
        for i, extra_ref in enumerate(extra_refs):
            columns = slice(i * part, (i + 1) * part)
            total = sum(t[:, columns].astype(F32) for t in term_refs)
            total = total + extra_ref[:kept, :].astype(F32)
            mixed_ref[:, columns] = total
            half_ref[:, columns] = total.astype(BF)

    return pl.pallas_call(
        kernel,
        out_shape=(
            jax.ShapeDtypeStruct((kept, width), F32),
            jax.ShapeDtypeStruct((kept, width), BF),
        ),
        compiler_params=params(),
    )(*terms, *extras)


def project(x_ref, weight_refs, tile, put):
    part = x_ref.shape[1] // len(weight_refs)
    for j in range(weight_refs[0].shape[1] // tile):
        columns = slice(j * tile, (j + 1) * tile)
        total = sum(
            jnp.dot(
                x_ref[:, i * part : (i + 1) * part], w[:, columns], preferred_element_type=F32
            )
            for i, w in enumerate(weight_refs)
        )
        put(columns, total.astype(BF))


def project_gate(blocks, extras, weights, tile=256):
    count = len(blocks)
    width = blocks[0].shape[1]
    rows = sum(block.shape[0] for block in blocks)
    size = rows // 8
    pieces = len(weights)
    hidden = weights[0].shape[1]
    kept = extras[0].shape[0] - 16

    def kernel(*refs):
        block_refs, refs = refs[:count], refs[count:]
        extra_refs, refs = refs[:pieces], refs[pieces:]
        weight_refs, (near_ref, far_ref, x_ref, square_ref) = refs[:pieces], refs[pieces:]
        gain = jnp.concatenate(
            [
                jnp.sum(e[...].astype(F32)[kept : kept + 3], axis=0, keepdims=True)
                for e in extra_refs
            ],
            axis=1,
        )
        done = 0
        for block_ref in block_refs:
            length = block_ref.shape[0]
            distance = distance_to(done // size)
            place = 2 * (distance & 3) + lax.shift_right_logical(distance, 2)
            spot = pl.ds(pl.multiple_of(place * size + done % size, length), length)
            block = block_ref[...].astype(F32)
            x_ref[spot, :] = (block * gain).astype(BF)
            square = jnp.sum(block * block, axis=1, keepdims=True)
            high = square.astype(BF).astype(F32)
            middle = (square - high).astype(BF).astype(F32)
            low = square - high - middle
            lane = lax.broadcasted_iota(jnp.int32, (length, 128), 1)
            square_ref[spot, :] = jnp.where(
                lane == 0, high, jnp.where(lane == 1, middle, jnp.where(lane == 2, low, 0.0))
            ).astype(BF)
            done += length

        def put(columns, value):
            for i in range(4):
                spot = slice(i * size, (i + 1) * size)
                near_ref[spot, columns] = value[2 * i * size : (2 * i + 1) * size]
                far_ref[spot, columns] = value[(2 * i + 1) * size : (2 * i + 2) * size]

        put(slice(hidden, hidden + 128), square_ref[...])
        project(x_ref, weight_refs, tile, put)

    half = jax.ShapeDtypeStruct((rows // 2, hidden + 128), BF)
    return pl.pallas_call(
        kernel,
        out_shape=(half, half, jax.ShapeDtypeStruct((rows, width), BF)),
        scratch_shapes=[pltpu.VMEM((rows, 128), BF)],
        compiler_params=params(24),
        cost_estimate=cost(2 * rows * width * hidden, 2 * width * hidden),
    )(*blocks, *extras, *weights)


def project_up(x, weights, tile=256):
    rows = x.shape[0] // 4
    hidden = weights[0].shape[1]
    pieces = len(weights)

    def kernel(x_ref, *refs):
        def put(columns, value):
            for i in range(4):
                refs[pieces + i][:, columns] = value[i * rows : (i + 1) * rows]

        project(x_ref, refs[:pieces], tile, put)

    return pl.pallas_call(
        kernel,
        out_shape=[jax.ShapeDtypeStruct((rows, hidden), BF)] * 4,
        compiler_params=params(24),
        cost_estimate=cost(8 * rows * x.shape[1] * hidden, 2 * x.shape[1] * hidden),
    )(x, *weights)


def fold(near, far, ups):
    rows, full = near.shape
    size = rows // 4
    hidden = ups[0].shape[1]

    def kernel(near_ref, far_ref, *refs):
        for i in range(4):
            spot = slice(i * size, (i + 1) * size)
            refs[4 + i][...] = (
                near_ref[spot, :].astype(F32) + far_ref[spot, :].astype(F32)
            ).astype(BF)
        for i in range(2):
            spot = slice(i * size, (i + 1) * size)
            refs[8 + i][...] = sum(u[spot, :].astype(F32) for u in refs[:4]).astype(BF)

    outs = pl.pallas_call(
        kernel,
        out_shape=[jax.ShapeDtypeStruct((size, full), BF)] * 4
        + [jax.ShapeDtypeStruct((size, hidden), BF)] * 2,
        compiler_params=params(24),
        cost_estimate=cost(10**6, 4 * 10**6),
    )(near, far, *ups)
    return outs[:4], outs[4], outs[5]


def activate(gates, ups, tile=256):
    rows, hidden = ups[0].shape
    count = len(gates)

    def kernel(*refs):
        gate_refs, up_refs, out_ref = refs[:count], refs[count:-1], refs[-1]
        square = sum(
            jnp.sum(g[:, hidden:].astype(F32), axis=1, keepdims=True) for g in gate_refs
        )
        inverse = lax.rsqrt(square / MODEL_WIDTH + epsilon)
        for j in range(hidden // tile):
            columns = slice(j * tile, (j + 1) * tile)
            gate = sum(g[:, columns].astype(F32) for g in gate_refs) * inverse
            up = sum(u[:, columns].astype(F32) for u in up_refs) * inverse
            out_ref[:, columns] = (gate / (1.0 + jnp.exp(-gate)) * up).astype(BF)

    return pl.pallas_call(
        kernel,
        out_shape=jax.ShapeDtypeStruct((rows, hidden), BF),
        compiler_params=params(24),
        cost_estimate=cost(10**6, 2 * 10**6),
    )(*gates, *ups)


def body(
    query,
    key_store_cache,
    value_store_cache,
    token_keys,
    token_values,
    pooled_block_keys,
    pooled_block_values,
    block_dst,
    block_row,
    ctx_len,
    residual,
    norm_gain,
    output_weight,
    w_gate,
    w_up,
    w_down,
):
    requests = query.shape[0]
    core = lax.axis_index("attn") & 1
    flat_dst = block_dst[:, 0]

    sent, piece, piece_far = place_blocks(
        flat_dst, pooled_block_keys, pooled_block_values, residual, norm_gain, requests
    )
    cached = cached_attention(
        ctx_len, query, key_store_cache, value_store_cache, token_keys, token_values
    )
    extras = [piece, swap(piece_far, 1)]
    weights = output_weight, w_gate, w_up, w_down
    sent, *weights = together(sent, *weights)
    received = lax.all_to_all(sent, "attn", split_axis=0, concat_axis=0, tiled=True)
    fars = [swap(w, 1) for w in weights]
    received, cached, *late = together(received, cached, *fars, *extras)
    fars, extras = late[:4], late[4:]

    attended = merge_received(
        query,
        cached,
        received.reshape(-1, received.shape[2]),
        flat_dst.reshape(1, -1),
        block_row.reshape(1, -1),
    )
    terms = product_sum(
        chip_gather(attended), (output_weight, fars[0]), lambda: lax.axis_index("ffn"), False
    )
    mixed, half_mixed = settle(terms, extras)
    gate_near, gate_far, scaled = project_gate(z_gather(half_mixed), extras, (w_gate, fars[1]))
    gate_far = swap(gate_far, 8)
    ups = x_scatter(project_up(scaled, (w_up, fars[2])))
    gates, up_near, up_far = fold(gate_near, gate_far, ups)
    up_far = swap(up_far, 8)
    activated = chip_gather(activate(x_scatter(gates), (up_near, up_far)))
    terms = product_sum(activated, (w_down, fars[3]), lambda: 0, True)

    layer_out = (mixed + sum(t.astype(F32) for t in terms)).astype(BF)
    half = layer_out.shape[1] // 2
    near = layer_out[:, :half]
    far = swap(layer_out[:, half:], 1)
    return jnp.where(
        core == 0, jnp.concatenate([near, far], axis=0), jnp.concatenate([far, near], axis=0)
    )


def solution(mesh):
    placed = (
        P(("grp", "attn"), "ffn"),
        P(("grp", "attn"), None, "ffn"),
        P(("grp", "attn"), None, "ffn"),
        P(("grp", "attn"), "ffn"),
        P(("grp", "attn"), "ffn"),
        P(("grp", "attn"), None, "ffn"),
        P(("grp", "attn"), None, "ffn"),
        P("grp", None),
        P("grp"),
        P(("grp", "attn")),
        P("grp", "attn"),
        P("attn"),
        P("ffn", "attn"),
        P("attn", "ffn"),
        P("attn", "ffn"),
        P("ffn", "attn"),
    )
    return jax.shard_map(
        body, mesh=mesh, in_specs=placed, out_specs=P(("grp", "ffn"), "attn"), check_vma=False
    )
```

```python
import jax
import jax.numpy as jnp
from jax import lax
from jax.experimental import pallas as pl
from jax.experimental.pallas import tpu as pltpu
from jax.sharding import PartitionSpec as P

MODEL_WIDTH = 8192
HEAD_SIZE = 128
HEADS = 8
CAP = 2
epsilon = 1e-05
BF = jnp.bfloat16
F32 = jnp.float32
NT = (((1,), (1,)), ((), ()))


def params(mebibytes=40):
    return pltpu.CompilerParams(vmem_limit_bytes=mebibytes * 1024 * 1024)


def whole(shape):
    return pl.BlockSpec(shape, lambda *_: (0,) * len(shape))


def cost(flops, size):
    return pl.CostEstimate(flops=flops, bytes_accessed=size, transcendentals=0)


def swap(value, bits):
    return lax.ppermute(value, "attn", [(a, a ^ bits) for a in range(16)])


def x_scatter(blocks):
    moved = [blocks[0]]
    for i in range(1, 4):
        pairs = [(a, (a & 9) | ((((a >> 1) + i) & 3) << 1)) for a in range(16)]
        moved.append(lax.ppermute(blocks[i], "attn", pairs))
    return moved


def chip_gather(value):
    blocks = []
    other = swap(value, 8)
    for start in (value, other):
        blocks.append(start)
        for step in range(1, 4):
            pairs = [(a, (a & 9) | ((((a >> 1) - step) & 3) << 1)) for a in range(16)]
            blocks.append(lax.ppermute(start, "attn", pairs))
    return blocks


def distance_to(chip):
    own = lax.shift_right_logical(lax.axis_index("attn"), 1)
    return ((chip ^ own) & 4) | ((chip - own) & 3)


def together(*values):
    return lax.optimization_barrier(values)


def z_shift(value, step):
    return lax.ppermute(value, "ffn", [(f, (f + step) % 8) for f in range(8)])


def added(moved, block):
    return (moved.astype(F32) + block.astype(F32)).astype(BF)


def z_scatter_sum(blocks, beside_last):
    rows = blocks[0].shape[0] // 2
    first = (
        z_shift(blocks[4][:rows], 2),
        z_shift(blocks[4][rows:], -2),
        z_shift(blocks[3], 1),
        z_shift(blocks[5], -1),
    )
    beside = blocks[1], blocks[7]
    if beside_last:
        *first, beside_right, beside_left = together(*first, *beside)
        beside = beside_right, beside_left
    top, bottom, from_left, from_right = first
    right = added(from_left, blocks[2])
    right = jnp.concatenate([added(top, right[:rows]), right[rows:]], axis=0)
    left = added(from_right, blocks[6])
    left = jnp.concatenate([left[:rows], added(bottom, left[rows:])], axis=0)
    return (
        z_shift(right, 2),
        z_shift(left, -2),
        z_shift(beside[0], 1),
        z_shift(beside[1], -1),
        blocks[0],
    )


def z_gather(value):
    rows = value.shape[0] // 2
    right, left = together(z_shift(value, 2), z_shift(value, -2))
    beside = z_shift(value, 1), z_shift(value, -1)
    top, bottom = z_shift(left[:rows], -2), z_shift(right[rows:], 2)
    far = z_shift(right, 1), z_shift(left, -1)
    return [value, beside[1], left, far[1], top, bottom, far[0], right, beside[0]]


def place_blocks(block_dst, pooled_keys, pooled_values, residual, norm_gain, kept):
    held, block_len, width = pooled_keys.shape
    slots = 16 * CAP
    columns = residual.shape[1]

    def kernel(dst_ref, k_ref, v_ref, gain_ref, res_ref, out_ref, *rest):
        piece_refs, buf, sems = rest[:2], rest[2], rest[3]
        index = lax.axis_index("attn")
        ffn_index = lax.axis_index("ffn")
        copies = []
        for i in range(2):
            start = pl.multiple_of((2 * ffn_index + ((index & 1) ^ i)) * kept, kept)
            copies.append(
                pltpu.make_async_copy(res_ref.at[pl.ds(start, kept)], buf.at[i], sems.at[i])
            )
            copies[i].start()
        first = index * held
        out_ref[...] = jnp.zeros_like(out_ref)
        dst = [dst_ref[first + j] for j in range(held)]
        for j in range(held):
            rank = jnp.int32(0)
            for i in range(j):
                rank = rank + jnp.where(dst[i] == dst[j], 1, 0)
            slot = dst[j] * CAP + jnp.minimum(rank, CAP - 1)
            out_ref[slot, :, :width] = k_ref[j]
            out_ref[slot, :, width:] = v_ref[j]
        gain = gain_ref[...]
        high = gain.astype(BF).astype(F32)
        middle = (gain - high).astype(BF).astype(F32)
        low = gain - high - middle
        row = lax.broadcasted_iota(jnp.int32, (16, columns), 0)
        gain_rows = jnp.where(
            row == 0, high, jnp.where(row == 1, middle, jnp.where(row == 2, low, 0.0))
        ).astype(BF)
        for i in range(2):
            copies[i].wait()
            piece_refs[i][:kept, :] = buf[i]
            piece_refs[i][kept:, :] = gain_rows

    return pl.pallas_call(
        kernel,
        out_shape=[jax.ShapeDtypeStruct((slots, block_len, 2 * width), BF)]
        + [jax.ShapeDtypeStruct((kept + 16, columns), BF)] * 2,
        in_specs=[
            pl.BlockSpec(memory_space=pltpu.SMEM),
            pl.BlockSpec(memory_space=pltpu.VMEM),
            pl.BlockSpec(memory_space=pltpu.VMEM),
            pl.BlockSpec(memory_space=pltpu.VMEM),
            pl.BlockSpec(memory_space=pltpu.HBM),
        ],
        out_specs=[pl.BlockSpec(memory_space=pltpu.VMEM)] * 3,
        scratch_shapes=[
            pltpu.VMEM((2, kept, columns), BF),
            pltpu.SemaphoreType.DMA((2,)),
        ],
        compiler_params=params(62),
    )(block_dst, pooled_keys, pooled_values, norm_gain.reshape(1, -1), residual)


def spread_heads(source_ref, target, count):
    for h in range(HEADS):
        target[pl.ds(h, count, stride=HEADS), :] = source_ref[
            :, h * HEAD_SIZE : (h + 1) * HEAD_SIZE
        ].astype(F32)


def cached_attention(ctx_len, query, keys, values, token_keys, token_values):
    requests, ctx_size, width = keys.shape
    step_rows = 32
    scale = HEAD_SIZE**-0.5
    hrows = step_rows * HEADS

    def kernel(
        ctx_ref, q_ref, k_ref, v_ref, tk_ref, tv_ref, out_ref, q_buf, tk_buf, tv_buf
    ):
        step = pl.program_id(0)
        spread_heads(q_ref, q_buf, step_rows)
        for h in range(HEADS):
            tk_buf[pl.ds(h, step_rows, stride=HEADS), :] = tk_ref[...].astype(F32)
            tv_buf[pl.ds(h, step_rows, stride=HEADS), :] = tv_ref[...].astype(F32)
        q_full = q_buf[...]
        q_half = q_full.astype(BF)
        scores = []
        spot = lax.broadcasted_iota(jnp.int32, (HEADS, ctx_size), 1)
        for b in range(step_rows):
            part = lax.dot_general(
                q_half[b * HEADS : (b + 1) * HEADS], k_ref[b], NT, preferred_element_type=F32
            )
            scores.append(
                jnp.where(spot < ctx_ref[step * step_rows + b], part * scale, -jnp.inf)
            )
        score_cache = jnp.concatenate(scores, axis=0)
        score_new = jnp.sum(q_full * tk_buf[...], axis=1, keepdims=True) * scale
        top = jnp.maximum(jnp.max(score_cache, axis=1, keepdims=True), score_new)
        exp_cache = jnp.exp(score_cache - top)
        exp_new = jnp.exp(score_new - top)
        total = jnp.sum(exp_cache, axis=1, keepdims=True) + exp_new
        prob_cache = exp_cache.astype(BF)
        prob_new = exp_new.astype(BF).astype(F32)
        attended = [
            jnp.dot(
                prob_cache[b * HEADS : (b + 1) * HEADS], v_ref[b], preferred_element_type=F32
            )
            for b in range(step_rows)
        ]
        out_ref[:, :width] = jnp.concatenate(attended, axis=0) + prob_new * tv_buf[...]
        lane = lax.broadcasted_iota(jnp.int32, (hrows, width), 1)
        out_ref[:, width:] = jnp.where(lane < width // 2, top, total)

    return pl.pallas_call(
        kernel,
        grid=(requests // step_rows,),
        out_shape=jax.ShapeDtypeStruct((requests * HEADS, 2 * width), F32),
        in_specs=[
            pl.BlockSpec(memory_space=pltpu.SMEM),
            pl.BlockSpec((step_rows, query.shape[1]), lambda i: (i, 0)),
            pl.BlockSpec((step_rows, ctx_size, width), lambda i: (i, 0, 0)),
            pl.BlockSpec((step_rows, ctx_size, width), lambda i: (i, 0, 0)),
            pl.BlockSpec((step_rows, width), lambda i: (i, 0)),
            pl.BlockSpec((step_rows, width), lambda i: (i, 0)),
        ],
        out_specs=pl.BlockSpec((hrows, 2 * width), lambda i: (i, 0)),
        scratch_shapes=[pltpu.VMEM((hrows, HEAD_SIZE), F32)] * 3,
        compiler_params=params(56),
        cost_estimate=cost(10**8, 7 * 10**6),
    )(ctx_len, query, keys, values, token_keys, token_values)


def merge_received(query, cached, received, dst, rows):
    requests = query.shape[0]
    width = cached.shape[1] // 2
    step_rows = 32
    slots = 16 * CAP
    recv_size = received.shape[0]
    block_len = recv_size // slots
    scale = HEAD_SIZE**-0.5
    hrows = step_rows * HEADS

    def kernel(
        q_ref, part_ref, r_ref, dst_ref, row_ref, out_ref, owner_ref, q_buf, o_buf
    ):
        step = pl.program_id(0)

        @pl.when(step == 0)
        def _():
            count = dst_ref.shape[1]
            held = 2 * count // slots
            hit = (dst_ref[...] == lax.axis_index("attn")).astype(F32)
            source = lax.broadcasted_iota(jnp.int32, (count, count), 0)
            target = lax.broadcasted_iota(jnp.int32, (count, count), 1)
            earlier = (source < target) & (source // held == target // held)
            rank = jnp.dot(
                jnp.broadcast_to(hit, (8, count)), earlier.astype(F32), preferred_element_type=F32
            )
            marked = hit * (row_ref[...].astype(F32) + 1.0)
            pool = lax.broadcasted_iota(jnp.int32, (count, recv_size), 0) // held
            slot = lax.broadcasted_iota(jnp.int32, (count, recv_size), 1) // block_len
            owner = jnp.full(owner_ref.shape, -1.0, F32)
            for i in range(CAP):
                chosen = jnp.where(jnp.abs(rank - i) < 0.5, marked, 0.0)
                owner = owner + jnp.dot(
                    chosen, (slot == pool * CAP + i).astype(F32), preferred_element_type=F32
                )
            owner_ref[...] = owner

        spread_heads(q_ref, q_buf, step_rows)
        score = (
            lax.dot_general(
                q_buf[...].astype(BF), r_ref[:, :width], NT, preferred_element_type=F32
            )
            * scale
        )
        request = (
            lax.broadcasted_iota(jnp.int32, (hrows, recv_size), 0) // HEADS + step * step_rows
        )
        score = jnp.where(request.astype(F32) == owner_ref[0:1, :], score, -jnp.inf)
        cached_top = part_ref[:, width : width + 1]
        top = jnp.maximum(cached_top, jnp.max(score, axis=1, keepdims=True))
        exp_recv = jnp.exp(score - top)
        shrink = jnp.exp(cached_top - top)
        total = part_ref[:, 2 * width - 1 :] * shrink + jnp.sum(exp_recv, axis=1, keepdims=True)
        o_buf[...] = (
            part_ref[:, :width] * shrink
            + jnp.dot(exp_recv.astype(BF), r_ref[:, width:], preferred_element_type=F32)
        ) / total
        for h in range(HEADS):
            head = o_buf[pl.ds(h, step_rows, stride=HEADS), :].astype(BF)
            out_ref[:, h * HEAD_SIZE : (h + 1) * HEAD_SIZE] = head

    part_spec = pl.BlockSpec((hrows, 2 * width), lambda i: (i, 0))
    return pl.pallas_call(
        kernel,
        grid=(requests // step_rows,),
        out_shape=jax.ShapeDtypeStruct((requests, query.shape[1]), BF),
        in_specs=[
            pl.BlockSpec((step_rows, query.shape[1]), lambda i: (i, 0)),
            part_spec,
            whole(received.shape),
            whole(dst.shape),
            whole(rows.shape),
        ],
        out_specs=pl.BlockSpec((step_rows, query.shape[1]), lambda i: (i, 0)),
        scratch_shapes=[
            pltpu.VMEM((8, recv_size), F32),
            pltpu.VMEM((hrows, HEAD_SIZE), F32),
            pltpu.VMEM((hrows, HEAD_SIZE), F32),
        ],
        compiler_params=params(24),
        cost_estimate=cost(10**8, 3 * 10**6),
    )(query, cached, received, dst, rows)


def side_by_side(x_blocks, weights, first, wanted, tile=256):
    rows, k = x_blocks[0].shape
    m = rows * len(wanted)
    n = weights[0].shape[1]
    count = len(weights)

    def kernel(*refs):
        block_refs, refs = refs[: len(x_blocks)], refs[len(x_blocks) :]
        weight_refs, (out_ref, x_ref) = refs[:count], refs[count:]
        start = first()
        for p, d in enumerate(wanted):
            index = distance_to((start + d) & 7)
            for i, block_ref in enumerate(block_refs):

                @pl.when(index == i)
                def _(p=p, block_ref=block_ref):
                    x_ref[p * rows : (p + 1) * rows, :] = block_ref[...]

        for i, weight_ref in enumerate(weight_refs):
            for j in range(n // tile):
                out_ref[:, :, i * n + j * tile : i * n + (j + 1) * tile] = (
                    jnp.dot(
                        x_ref[...],
                        weight_ref[:, j * tile : (j + 1) * tile],
                        preferred_element_type=F32,
                    )
                    .astype(BF)
                    .reshape(len(wanted), rows, tile)
                )

    return pl.pallas_call(
        kernel,
        out_shape=jax.ShapeDtypeStruct((len(wanted), rows, count * n), BF),
        scratch_shapes=[pltpu.VMEM((m, k), BF)],
        compiler_params=params(24),
        cost_estimate=cost(2 * m * count * n * k, 2 * (m * k + k * n * count + m * n * count)),
    )(*x_blocks, *weights)


def product_sum(x_blocks, weights, first, beside_last):
    far = side_by_side(x_blocks, weights, first, (3, 4, 5))
    near = side_by_side(x_blocks, weights, first, (0, 1, 2, 6, 7))
    return z_scatter_sum([*near[:3], *far, *near[3:]], beside_last)


def settle(terms, extras):
    kept, width = terms[0].shape
    part = width // len(extras)

    def kernel(*refs):
        term_refs, refs = refs[: len(terms)], refs[len(terms) :]
        extra_refs, (mixed_ref, half_ref) = refs[: len(extras)], refs[len(extras) :]
        for i, extra_ref in enumerate(extra_refs):
            columns = slice(i * part, (i + 1) * part)
            total = sum(t[:, columns].astype(F32) for t in term_refs)
            total = total + extra_ref[:kept, :].astype(F32)
            mixed_ref[:, columns] = total
            half_ref[:, columns] = total.astype(BF)

    return pl.pallas_call(
        kernel,
        out_shape=(
            jax.ShapeDtypeStruct((kept, width), F32),
            jax.ShapeDtypeStruct((kept, width), BF),
        ),
        compiler_params=params(),
    )(*terms, *extras)


def project(x_ref, weight_refs, tile, put):
    part = x_ref.shape[1] // len(weight_refs)
    for j in range(weight_refs[0].shape[1] // tile):
        columns = slice(j * tile, (j + 1) * tile)
        total = sum(
            jnp.dot(
                x_ref[:, i * part : (i + 1) * part], w[:, columns], preferred_element_type=F32
            )
            for i, w in enumerate(weight_refs)
        )
        put(columns, total.astype(BF))


def project_gate(blocks, extras, weights, tile=256):
    count = len(blocks)
    width = blocks[0].shape[1]
    rows = sum(block.shape[0] for block in blocks)
    size = rows // 8
    pieces = len(weights)
    hidden = weights[0].shape[1]
    kept = extras[0].shape[0] - 16

    def kernel(*refs):
        block_refs, refs = refs[:count], refs[count:]
        extra_refs, refs = refs[:pieces], refs[pieces:]
        weight_refs, (near_ref, far_ref, x_ref, square_ref) = refs[:pieces], refs[pieces:]
        gain = jnp.concatenate(
            [
                jnp.sum(e[...].astype(F32)[kept : kept + 3], axis=0, keepdims=True)
                for e in extra_refs
            ],
            axis=1,
        )
        done = 0
        for block_ref in block_refs:
            length = block_ref.shape[0]
            distance = distance_to(done // size)
            place = 2 * (distance & 3) + lax.shift_right_logical(distance, 2)
            spot = pl.ds(pl.multiple_of(place * size + done % size, length), length)
            block = block_ref[...].astype(F32)
            x_ref[spot, :] = (block * gain).astype(BF)
            square = jnp.sum(block * block, axis=1, keepdims=True)
            high = square.astype(BF).astype(F32)
            middle = (square - high).astype(BF).astype(F32)
            low = square - high - middle
            lane = lax.broadcasted_iota(jnp.int32, (length, 128), 1)
            square_ref[spot, :] = jnp.where(
                lane == 0, high, jnp.where(lane == 1, middle, jnp.where(lane == 2, low, 0.0))
            ).astype(BF)
            done += length

        def put(columns, value):
            for i in range(4):
                spot = slice(i * size, (i + 1) * size)
                near_ref[spot, columns] = value[2 * i * size : (2 * i + 1) * size]
                far_ref[spot, columns] = value[(2 * i + 1) * size : (2 * i + 2) * size]

        put(slice(hidden, hidden + 128), square_ref[...])
        project(x_ref, weight_refs, tile, put)

    half = jax.ShapeDtypeStruct((rows // 2, hidden + 128), BF)
    return pl.pallas_call(
        kernel,
        out_shape=(half, half, jax.ShapeDtypeStruct((rows, width), BF)),
        scratch_shapes=[pltpu.VMEM((rows, 128), BF)],
        compiler_params=params(24),
        cost_estimate=cost(2 * rows * width * hidden, 2 * width * hidden),
    )(*blocks, *extras, *weights)


def project_up(x, weights, tile=256):
    rows = x.shape[0] // 4
    hidden = weights[0].shape[1]
    pieces = len(weights)

    def kernel(x_ref, *refs):
        def put(columns, value):
            for i in range(4):
                refs[pieces + i][:, columns] = value[i * rows : (i + 1) * rows]

        project(x_ref, refs[:pieces], tile, put)

    return pl.pallas_call(
        kernel,
        out_shape=[jax.ShapeDtypeStruct((rows, hidden), BF)] * 4,
        compiler_params=params(24),
        cost_estimate=cost(8 * rows * x.shape[1] * hidden, 2 * x.shape[1] * hidden),
    )(x, *weights)


def fold(near, far, ups):
    rows, full = near.shape
    size = rows // 4
    hidden = ups[0].shape[1]

    def kernel(near_ref, far_ref, *refs):
        for i in range(4):
            spot = slice(i * size, (i + 1) * size)
            refs[4 + i][...] = (
                near_ref[spot, :].astype(F32) + far_ref[spot, :].astype(F32)
            ).astype(BF)
        for i in range(2):
            spot = slice(i * size, (i + 1) * size)
            refs[8 + i][...] = sum(u[spot, :].astype(F32) for u in refs[:4]).astype(BF)

    outs = pl.pallas_call(
        kernel,
        out_shape=[jax.ShapeDtypeStruct((size, full), BF)] * 4
        + [jax.ShapeDtypeStruct((size, hidden), BF)] * 2,
        compiler_params=params(24),
        cost_estimate=cost(10**6, 4 * 10**6),
    )(near, far, *ups)
    return outs[:4], outs[4], outs[5]


def activate(gates, ups, tile=256):
    rows, hidden = ups[0].shape
    count = len(gates)

    def kernel(*refs):
        gate_refs, up_refs, out_ref = refs[:count], refs[count:-1], refs[-1]
        square = sum(
            jnp.sum(g[:, hidden:].astype(F32), axis=1, keepdims=True) for g in gate_refs
        )
        inverse = lax.rsqrt(square / MODEL_WIDTH + epsilon)
        for j in range(hidden // tile):
            columns = slice(j * tile, (j + 1) * tile)
            gate = sum(g[:, columns].astype(F32) for g in gate_refs) * inverse
            up = sum(u[:, columns].astype(F32) for u in up_refs) * inverse
            out_ref[:, columns] = (gate / (1.0 + jnp.exp(-gate)) * up).astype(BF)

    return pl.pallas_call(
        kernel,
        out_shape=jax.ShapeDtypeStruct((rows, hidden), BF),
        compiler_params=params(24),
        cost_estimate=cost(10**6, 2 * 10**6),
    )(*gates, *ups)


def body(
    query,
    key_store_cache,
    value_store_cache,
    token_keys,
    token_values,
    pooled_block_keys,
    pooled_block_values,
    block_dst,
    block_row,
    ctx_len,
    residual,
    norm_gain,
    output_weight,
    w_gate,
    w_up,
    w_down,
):
    requests = query.shape[0]
    core = lax.axis_index("attn") & 1
    flat_dst = block_dst[:, 0]

    sent, piece, piece_far = place_blocks(
        flat_dst, pooled_block_keys, pooled_block_values, residual, norm_gain, requests
    )
    cached = cached_attention(
        ctx_len, query, key_store_cache, value_store_cache, token_keys, token_values
    )
    extras = [piece, swap(piece_far, 1)]
    weights = output_weight, w_gate, w_up, w_down
    sent, *weights = together(sent, *weights)
    received = lax.all_to_all(sent, "attn", split_axis=0, concat_axis=0, tiled=True)
    fars = [swap(w, 1) for w in weights]
    received, cached, *late = together(received, cached, *fars, *extras)
    fars, extras = late[:4], late[4:]

    attended = merge_received(
        query,
        cached,
        received.reshape(-1, received.shape[2]),
        flat_dst.reshape(1, -1),
        block_row.reshape(1, -1),
    )
    terms = product_sum(
        chip_gather(attended), (output_weight, fars[0]), lambda: lax.axis_index("ffn"), False
    )
    mixed, half_mixed = settle(terms, extras)
    gate_near, gate_far, scaled = project_gate(z_gather(half_mixed), extras, (w_gate, fars[1]))
    gate_far = swap(gate_far, 8)
    ups = x_scatter(project_up(scaled, (w_up, fars[2])))
    gates, up_near, up_far = fold(gate_near, gate_far, ups)
    up_far = swap(up_far, 8)
    activated = chip_gather(activate(x_scatter(gates), (up_near, up_far)))
    terms = product_sum(activated, (w_down, fars[3]), lambda: 0, True)

    layer_out = (mixed + sum(t.astype(F32) for t in terms)).astype(BF)
    half = layer_out.shape[1] // 2
    near = layer_out[:, :half]
    far = swap(layer_out[:, half:], 1)
    return jnp.where(
        core == 0, jnp.concatenate([near, far], axis=0), jnp.concatenate([far, near], axis=0)
    )


def solution(mesh):
    placed = (
        P(("grp", "attn"), "ffn"),
        P(("grp", "attn"), None, "ffn"),
        P(("grp", "attn"), None, "ffn"),
        P(("grp", "attn"), "ffn"),
        P(("grp", "attn"), "ffn"),
        P(("grp", "attn"), None, "ffn"),
        P(("grp", "attn"), None, "ffn"),
        P("grp", None),
        P("grp"),
        P(("grp", "attn")),
        P("grp", "attn"),
        P("attn"),
        P("ffn", "attn"),
        P("attn", "ffn"),
        P("attn", "ffn"),
        P("ffn", "attn"),
    )
    return jax.shard_map(
        body, mesh=mesh, in_specs=placed, out_specs=P(("grp", "ffn"), "attn"), check_vma=False
    )
```

```python
import jax
import jax.numpy as jnp
from jax import lax
from jax.experimental import pallas as pl
from jax.experimental.pallas import tpu as pltpu
from jax.sharding import PartitionSpec as P

MODEL_WIDTH = 8192
HEAD_SIZE = 128
HEADS = 8
CAP = 2
epsilon = 1e-05
BF = jnp.bfloat16
F32 = jnp.float32
NT = (((1,), (1,)), ((), ()))


def params(mebibytes=40):
    return pltpu.CompilerParams(vmem_limit_bytes=mebibytes * 1024 * 1024)


def whole(shape):
    return pl.BlockSpec(shape, lambda *_: (0,) * len(shape))


def cost(flops, size):
    return pl.CostEstimate(flops=flops, bytes_accessed=size, transcendentals=0)


def swap(value, bits):
    return lax.ppermute(value, "attn", [(a, a ^ bits) for a in range(16)])


def x_scatter(blocks):
    moved = [blocks[0]]
    for i in range(1, 4):
        pairs = [(a, (a & 9) | ((((a >> 1) + i) & 3) << 1)) for a in range(16)]
        moved.append(lax.ppermute(blocks[i], "attn", pairs))
    return moved


def chip_gather(value):
    blocks = []
    other = swap(value, 8)
    for start in (value, other):
        blocks.append(start)
        for step in range(1, 4):
            pairs = [(a, (a & 9) | ((((a >> 1) - step) & 3) << 1)) for a in range(16)]
            blocks.append(lax.ppermute(start, "attn", pairs))
    return blocks


def distance_to(chip):
    own = lax.shift_right_logical(lax.axis_index("attn"), 1)
    return ((chip ^ own) & 4) | ((chip - own) & 3)


def together(*values):
    return lax.optimization_barrier(values)


def z_shift(value, step):
    return lax.ppermute(value, "ffn", [(f, (f + step) % 8) for f in range(8)])


def added(moved, block):
    return (moved.astype(F32) + block.astype(F32)).astype(BF)


def z_scatter_sum(blocks, beside_last):
    rows = blocks[0].shape[0] // 2
    first = (
        z_shift(blocks[4][:rows], 2),
        z_shift(blocks[4][rows:], -2),
        z_shift(blocks[3], 1),
        z_shift(blocks[5], -1),
    )
    beside = blocks[1], blocks[7]
    if beside_last:
        *first, beside_right, beside_left = together(*first, *beside)
        beside = beside_right, beside_left
    top, bottom, from_left, from_right = first
    right = added(from_left, blocks[2])
    right = jnp.concatenate([added(top, right[:rows]), right[rows:]], axis=0)
    left = added(from_right, blocks[6])
    left = jnp.concatenate([left[:rows], added(bottom, left[rows:])], axis=0)
    return (
        z_shift(right, 2),
        z_shift(left, -2),
        z_shift(beside[0], 1),
        z_shift(beside[1], -1),
        blocks[0],
    )


def z_gather(value):
    right, left = together(z_shift(value, 2), z_shift(value, -2))
    beside = z_shift(value, 1), z_shift(value, -1)
    across = z_shift(right, 2)
    far = z_shift(right, 1), z_shift(left, -1)
    return [value, beside[1], left, far[1], across, far[0], right, beside[0]]


def place_blocks(block_dst, pooled_keys, pooled_values, residual, norm_gain, kept):
    held, block_len, width = pooled_keys.shape
    slots = 16 * CAP
    columns = residual.shape[1]

    def kernel(dst_ref, k_ref, v_ref, gain_ref, res_ref, out_ref, *rest):
        piece_refs, buf, sems = rest[:2], rest[2], rest[3]
        index = lax.axis_index("attn")
        ffn_index = lax.axis_index("ffn")
        copies = []
        for i in range(2):
            start = pl.multiple_of((2 * ffn_index + ((index & 1) ^ i)) * kept, kept)
            copies.append(
                pltpu.make_async_copy(res_ref.at[pl.ds(start, kept)], buf.at[i], sems.at[i])
            )
            copies[i].start()
        first = index * held
        out_ref[...] = jnp.zeros_like(out_ref)
        dst = [dst_ref[first + j] for j in range(held)]
        for j in range(held):
            rank = jnp.int32(0)
            for i in range(j):
                rank = rank + jnp.where(dst[i] == dst[j], 1, 0)
            slot = dst[j] * CAP + jnp.minimum(rank, CAP - 1)
            out_ref[slot, :, :width] = k_ref[j]
            out_ref[slot, :, width:] = v_ref[j]
        gain = gain_ref[...]
        high = gain.astype(BF).astype(F32)
        middle = (gain - high).astype(BF).astype(F32)
        low = gain - high - middle
        row = lax.broadcasted_iota(jnp.int32, (16, columns), 0)
        gain_rows = jnp.where(
            row == 0, high, jnp.where(row == 1, middle, jnp.where(row == 2, low, 0.0))
        ).astype(BF)
        for i in range(2):
            copies[i].wait()
            piece_refs[i][:kept, :] = buf[i]
            piece_refs[i][kept:, :] = gain_rows

    return pl.pallas_call(
        kernel,
        out_shape=[jax.ShapeDtypeStruct((slots, block_len, 2 * width), BF)]
        + [jax.ShapeDtypeStruct((kept + 16, columns), BF)] * 2,
        in_specs=[
            pl.BlockSpec(memory_space=pltpu.SMEM),
            pl.BlockSpec(memory_space=pltpu.VMEM),
            pl.BlockSpec(memory_space=pltpu.VMEM),
            pl.BlockSpec(memory_space=pltpu.VMEM),
            pl.BlockSpec(memory_space=pltpu.HBM),
        ],
        out_specs=[pl.BlockSpec(memory_space=pltpu.VMEM)] * 3,
        scratch_shapes=[
            pltpu.VMEM((2, kept, columns), BF),
            pltpu.SemaphoreType.DMA((2,)),
        ],
        compiler_params=params(62),
    )(block_dst, pooled_keys, pooled_values, norm_gain.reshape(1, -1), residual)


def spread_heads(source_ref, target, count):
    for h in range(HEADS):
        target[pl.ds(h, count, stride=HEADS), :] = source_ref[
            :, h * HEAD_SIZE : (h + 1) * HEAD_SIZE
        ].astype(F32)


def cached_attention(ctx_len, query, keys, values, token_keys, token_values):
    requests, ctx_size, width = keys.shape
    step_rows = 32
    scale = HEAD_SIZE**-0.5
    hrows = step_rows * HEADS

    def kernel(
        ctx_ref, q_ref, k_ref, v_ref, tk_ref, tv_ref, out_ref, q_buf, tk_buf, tv_buf
    ):
        step = pl.program_id(0)
        spread_heads(q_ref, q_buf, step_rows)
        for h in range(HEADS):
            tk_buf[pl.ds(h, step_rows, stride=HEADS), :] = tk_ref[...].astype(F32)
            tv_buf[pl.ds(h, step_rows, stride=HEADS), :] = tv_ref[...].astype(F32)
        q_full = q_buf[...]
        q_half = q_full.astype(BF)
        scores = []
        spot = lax.broadcasted_iota(jnp.int32, (HEADS, ctx_size), 1)
        for b in range(step_rows):
            part = lax.dot_general(
                q_half[b * HEADS : (b + 1) * HEADS], k_ref[b], NT, preferred_element_type=F32
            )
            scores.append(
                jnp.where(spot < ctx_ref[step * step_rows + b], part * scale, -jnp.inf)
            )
        score_cache = jnp.concatenate(scores, axis=0)
        score_new = jnp.sum(q_full * tk_buf[...], axis=1, keepdims=True) * scale
        top = jnp.maximum(jnp.max(score_cache, axis=1, keepdims=True), score_new)
        exp_cache = jnp.exp(score_cache - top)
        exp_new = jnp.exp(score_new - top)
        total = jnp.sum(exp_cache, axis=1, keepdims=True) + exp_new
        prob_cache = exp_cache.astype(BF)
        prob_new = exp_new.astype(BF).astype(F32)
        attended = [
            jnp.dot(
                prob_cache[b * HEADS : (b + 1) * HEADS], v_ref[b], preferred_element_type=F32
            )
            for b in range(step_rows)
        ]
        out_ref[:, :width] = jnp.concatenate(attended, axis=0) + prob_new * tv_buf[...]
        lane = lax.broadcasted_iota(jnp.int32, (hrows, width), 1)
        out_ref[:, width:] = jnp.where(lane < width // 2, top, total)

    return pl.pallas_call(
        kernel,
        grid=(requests // step_rows,),
        out_shape=jax.ShapeDtypeStruct((requests * HEADS, 2 * width), F32),
        in_specs=[
            pl.BlockSpec(memory_space=pltpu.SMEM),
            pl.BlockSpec((step_rows, query.shape[1]), lambda i: (i, 0)),
            pl.BlockSpec((step_rows, ctx_size, width), lambda i: (i, 0, 0)),
            pl.BlockSpec((step_rows, ctx_size, width), lambda i: (i, 0, 0)),
            pl.BlockSpec((step_rows, width), lambda i: (i, 0)),
            pl.BlockSpec((step_rows, width), lambda i: (i, 0)),
        ],
        out_specs=pl.BlockSpec((hrows, 2 * width), lambda i: (i, 0)),
        scratch_shapes=[pltpu.VMEM((hrows, HEAD_SIZE), F32)] * 3,
        compiler_params=params(56),
        cost_estimate=cost(10**8, 7 * 10**6),
    )(ctx_len, query, keys, values, token_keys, token_values)


def merge_received(query, cached, received, dst, rows):
    requests = query.shape[0]
    width = cached.shape[1] // 2
    step_rows = 32
    slots = 16 * CAP
    recv_size = received.shape[0]
    block_len = recv_size // slots
    scale = HEAD_SIZE**-0.5
    hrows = step_rows * HEADS

    def kernel(
        q_ref, part_ref, r_ref, dst_ref, row_ref, out_ref, owner_ref, q_buf, o_buf
    ):
        step = pl.program_id(0)

        @pl.when(step == 0)
        def _():
            count = dst_ref.shape[1]
            held = 2 * count // slots
            hit = (dst_ref[...] == lax.axis_index("attn")).astype(F32)
            source = lax.broadcasted_iota(jnp.int32, (count, count), 0)
            target = lax.broadcasted_iota(jnp.int32, (count, count), 1)
            earlier = (source < target) & (source // held == target // held)
            rank = jnp.dot(
                jnp.broadcast_to(hit, (8, count)), earlier.astype(F32), preferred_element_type=F32
            )
            marked = hit * (row_ref[...].astype(F32) + 1.0)
            pool = lax.broadcasted_iota(jnp.int32, (count, recv_size), 0) // held
            slot = lax.broadcasted_iota(jnp.int32, (count, recv_size), 1) // block_len
            owner = jnp.full(owner_ref.shape, -1.0, F32)
            for i in range(CAP):
                chosen = jnp.where(jnp.abs(rank - i) < 0.5, marked, 0.0)
                owner = owner + jnp.dot(
                    chosen, (slot == pool * CAP + i).astype(F32), preferred_element_type=F32
                )
            owner_ref[...] = owner

        spread_heads(q_ref, q_buf, step_rows)
        score = (
            lax.dot_general(
                q_buf[...].astype(BF), r_ref[:, :width], NT, preferred_element_type=F32
            )
            * scale
        )
        request = (
            lax.broadcasted_iota(jnp.int32, (hrows, recv_size), 0) // HEADS + step * step_rows
        )
        score = jnp.where(request.astype(F32) == owner_ref[0:1, :], score, -jnp.inf)
        cached_top = part_ref[:, width : width + 1]
        top = jnp.maximum(cached_top, jnp.max(score, axis=1, keepdims=True))
        exp_recv = jnp.exp(score - top)
        shrink = jnp.exp(cached_top - top)
        total = part_ref[:, 2 * width - 1 :] * shrink + jnp.sum(exp_recv, axis=1, keepdims=True)
        o_buf[...] = (
            part_ref[:, :width] * shrink
            + jnp.dot(exp_recv.astype(BF), r_ref[:, width:], preferred_element_type=F32)
        ) / total
        for h in range(HEADS):
            head = o_buf[pl.ds(h, step_rows, stride=HEADS), :].astype(BF)
            out_ref[:, h * HEAD_SIZE : (h + 1) * HEAD_SIZE] = head

    part_spec = pl.BlockSpec((hrows, 2 * width), lambda i: (i, 0))
    return pl.pallas_call(
        kernel,
        grid=(requests // step_rows,),
        out_shape=jax.ShapeDtypeStruct((requests, query.shape[1]), BF),
        in_specs=[
            pl.BlockSpec((step_rows, query.shape[1]), lambda i: (i, 0)),
            part_spec,
            whole(received.shape),
            whole(dst.shape),
            whole(rows.shape),
        ],
        out_specs=pl.BlockSpec((step_rows, query.shape[1]), lambda i: (i, 0)),
        scratch_shapes=[
            pltpu.VMEM((8, recv_size), F32),
            pltpu.VMEM((hrows, HEAD_SIZE), F32),
            pltpu.VMEM((hrows, HEAD_SIZE), F32),
        ],
        compiler_params=params(24),
        cost_estimate=cost(10**8, 3 * 10**6),
    )(query, cached, received, dst, rows)


def side_by_side(x_blocks, weights, first, wanted, tile=256):
    rows, k = x_blocks[0].shape
    m = rows * len(wanted)
    n = weights[0].shape[1]
    count = len(weights)

    def kernel(*refs):
        block_refs, refs = refs[: len(x_blocks)], refs[len(x_blocks) :]
        weight_refs, (out_ref, x_ref) = refs[:count], refs[count:]
        start = first()
        for p, d in enumerate(wanted):
            index = distance_to((start + d) & 7)
            for i, block_ref in enumerate(block_refs):

                @pl.when(index == i)
                def _(p=p, block_ref=block_ref):
                    x_ref[p * rows : (p + 1) * rows, :] = block_ref[...]

        for i, weight_ref in enumerate(weight_refs):
            for j in range(n // tile):
                out_ref[:, :, i * n + j * tile : i * n + (j + 1) * tile] = (
                    jnp.dot(
                        x_ref[...],
                        weight_ref[:, j * tile : (j + 1) * tile],
                        preferred_element_type=F32,
                    )
                    .astype(BF)
                    .reshape(len(wanted), rows, tile)
                )

    return pl.pallas_call(
        kernel,
        out_shape=jax.ShapeDtypeStruct((len(wanted), rows, count * n), BF),
        scratch_shapes=[pltpu.VMEM((m, k), BF)],
        compiler_params=params(24),
        cost_estimate=cost(2 * m * count * n * k, 2 * (m * k + k * n * count + m * n * count)),
    )(*x_blocks, *weights)


def product_sum(x_blocks, weights, first, beside_last):
    far = side_by_side(x_blocks, weights, first, (3, 4, 5))
    near = side_by_side(x_blocks, weights, first, (0, 1, 2, 6, 7))
    return z_scatter_sum([*near[:3], *far, *near[3:]], beside_last)


def settle(terms, extras):
    kept, width = terms[0].shape
    part = width // len(extras)

    def kernel(*refs):
        term_refs, refs = refs[: len(terms)], refs[len(terms) :]
        extra_refs, (mixed_ref, half_ref) = refs[: len(extras)], refs[len(extras) :]
        for i, extra_ref in enumerate(extra_refs):
            columns = slice(i * part, (i + 1) * part)
            total = sum(t[:, columns].astype(F32) for t in term_refs)
            total = total + extra_ref[:kept, :].astype(F32)
            mixed_ref[:, columns] = total
            half_ref[:, columns] = total.astype(BF)

    return pl.pallas_call(
        kernel,
        out_shape=(
            jax.ShapeDtypeStruct((kept, width), F32),
            jax.ShapeDtypeStruct((kept, width), BF),
        ),
        compiler_params=params(),
    )(*terms, *extras)


def project(x_ref, weight_refs, tile, put):
    part = x_ref.shape[1] // len(weight_refs)
    for j in range(weight_refs[0].shape[1] // tile):
        columns = slice(j * tile, (j + 1) * tile)
        total = sum(
            jnp.dot(
                x_ref[:, i * part : (i + 1) * part], w[:, columns], preferred_element_type=F32
            )
            for i, w in enumerate(weight_refs)
        )
        put(columns, total.astype(BF))


def project_gate(blocks, extras, weights, tile=256):
    count = len(blocks)
    width = blocks[0].shape[1]
    rows = sum(block.shape[0] for block in blocks)
    size = rows // 8
    pieces = len(weights)
    hidden = weights[0].shape[1]
    kept = extras[0].shape[0] - 16

    def kernel(*refs):
        block_refs, refs = refs[:count], refs[count:]
        extra_refs, refs = refs[:pieces], refs[pieces:]
        weight_refs, (near_ref, far_ref, x_ref, square_ref) = refs[:pieces], refs[pieces:]
        gain = jnp.concatenate(
            [
                jnp.sum(e[...].astype(F32)[kept : kept + 3], axis=0, keepdims=True)
                for e in extra_refs
            ],
            axis=1,
        )
        done = 0
        for block_ref in block_refs:
            length = block_ref.shape[0]
            distance = distance_to(done // size)
            place = 2 * (distance & 3) + lax.shift_right_logical(distance, 2)
            spot = pl.ds(pl.multiple_of(place * size + done % size, length), length)
            block = block_ref[...].astype(F32)
            x_ref[spot, :] = (block * gain).astype(BF)
            square = jnp.sum(block * block, axis=1, keepdims=True)
            high = square.astype(BF).astype(F32)
            middle = (square - high).astype(BF).astype(F32)
            low = square - high - middle
            lane = lax.broadcasted_iota(jnp.int32, (length, 128), 1)
            square_ref[spot, :] = jnp.where(
                lane == 0, high, jnp.where(lane == 1, middle, jnp.where(lane == 2, low, 0.0))
            ).astype(BF)
            done += length

        def put(columns, value):
            for i in range(4):
                spot = slice(i * size, (i + 1) * size)
                near_ref[spot, columns] = value[2 * i * size : (2 * i + 1) * size]
                far_ref[spot, columns] = value[(2 * i + 1) * size : (2 * i + 2) * size]

        put(slice(hidden, hidden + 128), square_ref[...])
        project(x_ref, weight_refs, tile, put)

    half = jax.ShapeDtypeStruct((rows // 2, hidden + 128), BF)
    return pl.pallas_call(
        kernel,
        out_shape=(half, half, jax.ShapeDtypeStruct((rows, width), BF)),
        scratch_shapes=[pltpu.VMEM((rows, 128), BF)],
        compiler_params=params(24),
        cost_estimate=cost(2 * rows * width * hidden, 2 * width * hidden),
    )(*blocks, *extras, *weights)


def project_up(x, weights, tile=256):
    rows = x.shape[0] // 4
    hidden = weights[0].shape[1]
    pieces = len(weights)

    def kernel(x_ref, *refs):
        def put(columns, value):
            for i in range(4):
                refs[pieces + i][:, columns] = value[i * rows : (i + 1) * rows]

        project(x_ref, refs[:pieces], tile, put)

    return pl.pallas_call(
        kernel,
        out_shape=[jax.ShapeDtypeStruct((rows, hidden), BF)] * 4,
        compiler_params=params(24),
        cost_estimate=cost(8 * rows * x.shape[1] * hidden, 2 * x.shape[1] * hidden),
    )(x, *weights)


def fold(near, far, ups):
    rows, full = near.shape
    size = rows // 4
    hidden = ups[0].shape[1]

    def kernel(near_ref, far_ref, *refs):
        for i in range(4):
            spot = slice(i * size, (i + 1) * size)
            refs[4 + i][...] = (
                near_ref[spot, :].astype(F32) + far_ref[spot, :].astype(F32)
            ).astype(BF)
        for i in range(2):
            spot = slice(i * size, (i + 1) * size)
            refs[8 + i][...] = sum(u[spot, :].astype(F32) for u in refs[:4]).astype(BF)

    outs = pl.pallas_call(
        kernel,
        out_shape=[jax.ShapeDtypeStruct((size, full), BF)] * 4
        + [jax.ShapeDtypeStruct((size, hidden), BF)] * 2,
        compiler_params=params(24),
        cost_estimate=cost(10**6, 4 * 10**6),
    )(near, far, *ups)
    return outs[:4], outs[4], outs[5]


def activate(gates, ups, tile=256):
    rows, hidden = ups[0].shape
    count = len(gates)

    def kernel(*refs):
        gate_refs, up_refs, out_ref = refs[:count], refs[count:-1], refs[-1]
        square = sum(
            jnp.sum(g[:, hidden:].astype(F32), axis=1, keepdims=True) for g in gate_refs
        )
        inverse = lax.rsqrt(square / MODEL_WIDTH + epsilon)
        for j in range(hidden // tile):
            columns = slice(j * tile, (j + 1) * tile)
            gate = sum(g[:, columns].astype(F32) for g in gate_refs) * inverse
            up = sum(u[:, columns].astype(F32) for u in up_refs) * inverse
            out_ref[:, columns] = (gate / (1.0 + jnp.exp(-gate)) * up).astype(BF)

    return pl.pallas_call(
        kernel,
        out_shape=jax.ShapeDtypeStruct((rows, hidden), BF),
        compiler_params=params(24),
        cost_estimate=cost(10**6, 2 * 10**6),
    )(*gates, *ups)


def body(
    query,
    key_store_cache,
    value_store_cache,
    token_keys,
    token_values,
    pooled_block_keys,
    pooled_block_values,
    block_dst,
    block_row,
    ctx_len,
    residual,
    norm_gain,
    output_weight,
    w_gate,
    w_up,
    w_down,
):
    requests = query.shape[0]
    core = lax.axis_index("attn") & 1
    flat_dst = block_dst[:, 0]

    sent, piece, piece_far = place_blocks(
        flat_dst, pooled_block_keys, pooled_block_values, residual, norm_gain, requests
    )
    cached = cached_attention(
        ctx_len, query, key_store_cache, value_store_cache, token_keys, token_values
    )
    extras = [piece, swap(piece_far, 1)]
    weights = output_weight, w_gate, w_up, w_down
    sent, *weights = together(sent, *weights)
    received = lax.all_to_all(sent, "attn", split_axis=0, concat_axis=0, tiled=True)
    fars = [swap(w, 1) for w in weights]
    received, cached, *late = together(received, cached, *fars, *extras)
    fars, extras = late[:4], late[4:]

    attended = merge_received(
        query,
        cached,
        received.reshape(-1, received.shape[2]),
        flat_dst.reshape(1, -1),
        block_row.reshape(1, -1),
    )
    terms = product_sum(
        chip_gather(attended), (output_weight, fars[0]), lambda: lax.axis_index("ffn"), False
    )
    mixed, half_mixed = settle(terms, extras)
    gate_near, gate_far, scaled = project_gate(z_gather(half_mixed), extras, (w_gate, fars[1]))
    gate_far = swap(gate_far, 8)
    ups = x_scatter(project_up(scaled, (w_up, fars[2])))
    gates, up_near, up_far = fold(gate_near, gate_far, ups)
    up_far = swap(up_far, 8)
    activated = chip_gather(activate(x_scatter(gates), (up_near, up_far)))
    terms = product_sum(activated, (w_down, fars[3]), lambda: 0, True)

    layer_out = (mixed + sum(t.astype(F32) for t in terms)).astype(BF)
    half = layer_out.shape[1] // 2
    near = layer_out[:, :half]
    far = swap(layer_out[:, half:], 1)
    return jnp.where(
        core == 0, jnp.concatenate([near, far], axis=0), jnp.concatenate([far, near], axis=0)
    )


def solution(mesh):
    placed = (
        P(("grp", "attn"), "ffn"),
        P(("grp", "attn"), None, "ffn"),
        P(("grp", "attn"), None, "ffn"),
        P(("grp", "attn"), "ffn"),
        P(("grp", "attn"), "ffn"),
        P(("grp", "attn"), None, "ffn"),
        P(("grp", "attn"), None, "ffn"),
        P("grp", None),
        P("grp"),
        P(("grp", "attn")),
        P("grp", "attn"),
        P("attn"),
        P("ffn", "attn"),
        P("attn", "ffn"),
        P("attn", "ffn"),
        P("ffn", "attn"),
    )
    return jax.shard_map(
        body, mesh=mesh, in_specs=placed, out_specs=P(("grp", "ffn"), "attn"), check_vma=False
    )
```
